512 devices in a mesh: dp: 16 (over z_hi, x, core), seq: 32 (over y, z_lo).
Axes of the slice: x: 4, y: 4, z: 16 (z_hi: 2, z_lo: 8; z = z_hi * 8 + z_lo), core: 2. Of those that a mesh axis runs over, the one named last changes fastest.
Arguments:
- ssm_input: bfloat16 [65536, 1024], P(('dp', 'seq')), may hold values from -6 to 6
- gate_input: bfloat16 [65536, 1024], P(('dp', 'seq')), may hold values from -6 to 6
- b_proj: bfloat16 [65536, 128], P(('dp', 'seq')), may hold values from -6 to 6
- c_proj: bfloat16 [65536, 128], P(('dp', 'seq')), may hold values from -0.5 to 0.5
- dt_raw: float32 [65536, 16], P(('dp', 'seq')), may hold values from -5 to 5
- cotangent: bfloat16 [65536, 1024], P(('dp', 'seq')), may hold values from -6 to 6
- a_log: float32 [16], replicated, may hold values from -11 to -3
- dt_bias: float32 [16], replicated, may hold values from -2.5 to 2.5
- d_skip: float32 [16], replicated, may hold values from -3 to 3
- norm_gain: float32 [1024], replicated, may hold values from 0.5 to 1.5
- probe_a: float32 [16], replicated, may hold values from -3 to 3
- probe_dt: float32 [16], replicated, may hold values from -3 to 3
- probe_skip: float32 [16], replicated, may hold values from -3 to 3
- probe_gain: float32 [1024], replicated, may hold values from -3 to 3
Outputs:
- hvp_input: float32 [65536, 1024], P(('dp', 'seq'))
- hvp_a: float32 [16], replicated
- hvp_dt: float32 [16], replicated
- hvp_skip: float32 [16], replicated
- hvp_gain: float32 [1024], replicated
The draws below stay inside these ranges and needn't reach their ends.
All inputs are finite; a program needn't handle non-finite values.
Results may differ from the reference program's by a relative error of at most 0.0004.
Values sent between devices are 32-bit elements; how exact they have to be, the bound alone decides.
No kernel may reach another device: no remote copies, remote signals or barrier semaphores. Data moves between devices by JAX's collectives and lax.ppermute only.
A program may use at most 128 MiB of HBM per device.

```python
import math
import jax
import jax.numpy as jnp
from jax import lax

HEADS = 16
HEADDIM = 64
STATE = 128
TOK_DEV = 128
CH = 1024
SEQLEN = 4096
SEQS = 16
TOKENS = 65536
N_SEQ = 32


def draw_a_log(key, part):
    key = jax.random.fold_in(key, 11)
    key_pick, key_slow, key_fast = jax.random.split(key, 3)
    fast_share = 0.5
    picks = jax.random.uniform(key_pick, (HEADS,), jnp.float32)
    slow = jax.random.uniform(key_slow, (HEADS,), jnp.float32, jnp.log(0.5), jnp.log(1.5)) - jnp.log(0.8 * SEQLEN)
    fast = jax.random.uniform(key_fast, (HEADS,), jnp.float32, jnp.log(0.02), jnp.log(0.039)) - jnp.log(0.8)
    return jnp.where(picks < fast_share, fast, slow).astype(jnp.float32)


def shard_levels(rng, extent, cuts, least, top_value):
    loudness, own = 1.0, jax.random.fold_in(rng, 6)
    for position, parts in cuts:
        draws = jnp.exp(jax.random.uniform(jax.random.fold_in(own, position), (parts,), jnp.float32, least / len(cuts), top_value / len(cuts)))
        loudness = loudness * jnp.repeat(draws, extent[position] // parts).reshape([-1 if axis == position else 1 for axis in range(len(extent))])
    return loudness


def noise(own_key, dims, deviation, bound, shards=(), dtype=jnp.bfloat16):
    result = deviation * jax.random.normal(own_key, dims, jnp.float32)
    if shards:
        result = result * shard_levels(own_key, dims, shards, -0.22, 0.18)
    return jnp.clip(result, -bound, bound).astype(dtype)


def setup_inputs(seed: int = 0) -> dict:
    splits = jax.random.split(jax.random.key(seed), 15)
    return {
        "ssm_input": noise(splits[0], (TOKENS, CH), 1.0, 6.0, ((0, 512),)),
        "gate_input": noise(splits[1], (TOKENS, CH), 1.0, 6.0, ((0, 512),)),
        "b_proj": noise(splits[2], (TOKENS, STATE), 1.0, 6.0, ((0, 512),)),
        "c_proj": noise(splits[3], (TOKENS, STATE), STATE ** -0.5, 0.5, ((0, 512),)),
        "dt_raw": noise(splits[4], (TOKENS, HEADS), 1.0, 5.0, ((0, 512),), jnp.float32),
        "cotangent": noise(splits[5], (TOKENS, CH), 1.0, 6.0, ((0, 512),)),
        "a_log": draw_a_log(jax.random.fold_in(splits[14], 71), 0),
        "dt_bias": noise(splits[7], (HEADS,), 0.5, 2.5, (), jnp.float32),
        "d_skip": noise(splits[8], (HEADS,), 1.0, 3.0, (), jnp.float32),
        "norm_gain": jnp.clip(jax.random.uniform(splits[9], (CH,), jnp.float32, 0.5, 1.5), 0.5, 1.5),
        "probe_a": noise(splits[10], (HEADS,), 1.0, 3.0, (), jnp.float32),
        "probe_dt": noise(splits[11], (HEADS,), 1.0, 3.0, (), jnp.float32),
        "probe_skip": noise(splits[12], (HEADS,), 1.0, 3.0, (), jnp.float32),
        "probe_gain": noise(splits[13], (CH,), 1.0, 3.0, (), jnp.float32),
    }


PRECISE = lax.Precision.HIGHEST
EPS = 1e-05

def block_state(params, x_vals, b_vals, dt_vals):
    a_log, dt_bias = (params[0], params[1])
    steps_dt = jax.nn.softplus(dt_vals + dt_bias[None, :])
    rates = -jnp.exp(a_log)[None, :] * steps_dt
    cum_decay = jnp.cumsum(rates, axis=0)
    totals = cum_decay[-1]
    tail_weight = jnp.exp(totals[None, :] - cum_decay) * steps_dt
    n_heads = a_log.shape[0]
    x_heads = x_vals.reshape(x_vals.shape[0], n_heads, -1)
    states = jnp.einsum('sh,shp,sn->hpn', tail_weight, x_heads, b_vals, precision=PRECISE)
    return (totals, states, steps_dt, cum_decay)

def block_out(params, x_vals, z_vals, b_vals, c_vals, dt_vals, h_in):
    a_log, dt_bias, d_skip, norm_gain = params
    totals, states, steps_dt, cum_decay = block_state(params, x_vals, b_vals, dt_vals)
    n_rows = x_vals.shape[0]
    n_heads = a_log.shape[0]
    x_heads = x_vals.reshape(n_rows, n_heads, -1)
    scores = jnp.dot(c_vals, b_vals.T, precision=PRECISE)
    cum_heads = cum_decay.T
    gap_decay = cum_heads[:, :, None] - cum_heads[:, None, :]
    causal = (jnp.arange(n_rows)[:, None] >= jnp.arange(n_rows)[None, :])[None]
    decays = jnp.where(causal, jnp.exp(jnp.where(causal, gap_decay, 0.0)), 0.0)
    weights = decays * scores[None] * steps_dt.T[:, None, :]
    mixed_y = jnp.einsum('hts,shp->thp', weights, x_heads, precision=PRECISE)
    mixed_y = mixed_y + jnp.exp(cum_decay)[:, :, None] * jnp.einsum('tn,hpn->thp', c_vals, h_in, precision=PRECISE)
    mixed_y = mixed_y + d_skip[None, :, None] * x_heads
    gated_y = mixed_y.reshape(n_rows, -1) * jax.nn.silu(z_vals)
    inv_rms = lax.rsqrt(lax.optimization_barrier(jnp.mean(gated_y * gated_y, axis=1, keepdims=True)) + EPS)
    normed = gated_y * inv_rms * norm_gain[None, :]
    h_out = jnp.exp(totals)[:, None, None] * h_in + states
    return (normed, h_out)

def reference(ssm_input, gate_input, b_proj, c_proj, dt_raw, cotangent, a_log, dt_bias, d_skip, norm_gain, probe_a, probe_dt, probe_skip, probe_gain):
    params = (a_log, dt_bias, d_skip, norm_gain)
    probe = (probe_a, probe_dt, probe_skip, probe_gain)
    shape_rows = (SEQS, N_SEQ, TOK_DEV)
    x_all = ssm_input.astype(jnp.float32).reshape(shape_rows + (CH,))
    z_all = gate_input.astype(jnp.float32).reshape(shape_rows + (CH,))
    b_all = b_proj.astype(jnp.float32).reshape(shape_rows + (STATE,))
    c_all = c_proj.astype(jnp.float32).reshape(shape_rows + (STATE,))
    dt_all = dt_raw.reshape(shape_rows + (HEADS,))
    cot_all = cotangent.astype(jnp.float32).reshape(shape_rows + (CH,))

    def seq_loss(prm, x_seq, z_seq, b_seq, c_seq, dt_seq, cot_seq):

        def advance(h_carry, blocks):
            x_blk, z_blk, b_blk, c_blk, dt_blk, cot_blk = blocks
            normed, h_next = block_out(prm, x_blk, z_blk, b_blk, c_blk, dt_blk, h_carry)
            return (h_next, jnp.sum(normed * cot_blk))
        h_start = jnp.zeros((HEADS, HEADDIM, STATE), jnp.float32)
        h_final, pieces = lax.scan(advance, h_start, (x_seq, z_seq, b_seq, c_seq, dt_seq, cot_seq))
        return jnp.sum(pieces)

    def one_seq(blocks):
        x_seq, z_seq, b_seq, c_seq, dt_seq, cot_seq = blocks

        def grad_fn(prm):
            return jax.grad(seq_loss, argnums=(0, 1))(prm, x_seq, z_seq, b_seq, c_seq, dt_seq, cot_seq)
        primal, tangent = jax.jvp(grad_fn, (params,), (probe,))
        return tangent
    tangent_all = lax.map(one_seq, (x_all, z_all, b_all, c_all, dt_all, cot_all))
    param_tan, input_tan = tangent_all
    factor = 1.0 / math.sqrt(TOKENS)
    hvp_input = input_tan.reshape(TOKENS, CH)
    return (hvp_input, lax.optimization_barrier(jnp.sum(param_tan[0], axis=0)) * factor, lax.optimization_barrier(jnp.sum(param_tan[1], axis=0)) * factor, lax.optimization_barrier(jnp.sum(param_tan[2], axis=0)) * factor, lax.optimization_barrier(jnp.sum(param_tan[3], axis=0)) * factor)
```

```python
import functools
import math

import jax
import jax.numpy as jnp
from jax import lax
from jax.experimental import pallas as pl
from jax.experimental.pallas import tpu as pltpu
from jax.sharding import Mesh, PartitionSpec as P

F32, BF16 = jnp.float32, jnp.bfloat16
EPS = 1e-05
T = 128
N = 128
HD = 64
HEADS = 16
CH = 1024
BLK = 4
HPD = HEADS // BLK
CPD = HPD * HD
ROWS = BLK * HPD
SEGS = 8
CPS = CPD // SEGS
PARAMS = 6
X_ROWS = CPD + N + HPD + PARAMS * HPD + 4
G_ROWS = 2 * CPD + T + 8
M_ROWS = 2 * CPS + 8
VMEM = 48 * 1024 * 1024

(K_C, K_DC, K_DT, K_DDT, K_W, K_DW, K_TAIL, K_SG, K_DSG, K_F0, K_F1, K_G, K_DG, K_F0T, K_F1T, K_D, K_DD) = range(17)
TABLE = 17


def split(a):
    hi = a.astype(BF16)
    return hi, (a - hi.astype(F32)).astype(BF16)


def mm(a, b):
    return lax.dot_general(a, b, (((1,), (0,)), ((), ())), preferred_element_type=F32)


def mmt(a, b):
    return lax.dot_general(a, b, (((1,), (1,)), ((), ())), preferred_element_type=F32)


def heads_rows(table, k, b):
    return jnp.concatenate(
        [jnp.broadcast_to(table[k, b * HPD + h : b * HPD + h + 1, :], (HD, T)) for h in range(HPD)], axis=0
    )


def pack_x_kernel(x_ref, b_ref, dt_ref, *rest):
    prm, o_ref = rest[:PARAMS], rest[PARAMS]
    for j in range(BLK):
        for i in range(CPD // 128):
            lo = j * CPD + i * 128
            o_ref[j, i * 128 : (i + 1) * 128, :] = x_ref[:, lo : lo + 128].astype(F32).T
        o_ref[j, CPD : CPD + N, :] = b_ref[...].astype(F32)
        at = CPD + N
        o_ref[j, at : at + HPD, :] = dt_ref[j * HPD : (j + 1) * HPD, :]
        at += HPD
        for k in range(PARAMS):
            for h in range(HPD):
                o_ref[j, at : at + 1, :] = jnp.full((1, T), prm[k][j * HPD + h], F32)
                at += 1
        o_ref[j, at : at + 4, :] = jnp.zeros((4, T), F32)


def pack_g_kernel(z_ref, cot_ref, c_ref, gain_ref, dgain_ref, o_ref):
    halves = CPD // 128
    for j in range(BLK):
        for n, ref in enumerate((z_ref, cot_ref)):
            for i in range(halves):
                lo = j * CPD + i * 128
                at = n * CPD + i * 128
                o_ref[j, at : at + 128, :] = ref[:, lo : lo + 128].astype(F32).T
        o_ref[j, 2 * CPD : 2 * CPD + T, :] = c_ref[...].astype(F32)
        at = 2 * CPD + T
        o_ref[j, at : at + halves, :] = gain_ref[j * halves : (j + 1) * halves, :]
        o_ref[j, at + halves : at + 2 * halves, :] = dgain_ref[j * halves : (j + 1) * halves, :]
        o_ref[j, at + 2 * halves : at + 8, :] = jnp.zeros((8 - 2 * halves, 128), F32)


def write_message(msg_ref, total, d_total, table):
    for j in range(SEGS):
        h = j * CPS // HD
        msg_ref[j, 0:CPS, :] = total[j * CPS : (j + 1) * CPS]
        msg_ref[j, CPS : 2 * CPS, :] = d_total[j * CPS : (j + 1) * CPS]
        g, dg = None, None
        for b in range(BLK):
            r = b * HPD + h
            g_b, dg_b = table[K_G, r : r + 1, :], table[K_DG, r : r + 1, :]
            g, dg = (g_b, dg_b) if g is None else (g + g_b, dg + dg_b)
        msg_ref[j, 2 * CPS : 2 * CPS + 1, :] = g
        msg_ref[j, 2 * CPS + 1 : 2 * CPS + 2, :] = dg
        msg_ref[j, 2 * CPS + 2 : M_ROWS, :] = jnp.zeros((M_ROWS - 2 * CPS - 2, T), F32)


def state_kernel(r_ref, table_ref, cols_ref, s_ref, msg_ref):
    at = CPD + N

    def gather(lo):
        return jnp.concatenate([r_ref[b, lo : lo + HPD, :] for b in range(BLK)], axis=0)

    raw = gather(at)
    a_log, dt_bias, d_skip, p_a, p_dt, p_skip = [gather(at + HPD * (1 + k)) for k in range(PARAMS)]
    pre = raw + dt_bias
    dt = jnp.maximum(pre, 0.0) + jnp.log1p(jnp.exp(-jnp.abs(pre)))
    sg = 1.0 / (1.0 + jnp.exp(-pre))
    dsg = sg * (1.0 - sg) * p_dt
    ddt = sg * p_dt
    a = -jnp.exp(a_log)
    da = a * p_a
    before = lax.broadcasted_iota(jnp.int32, (T, T), 0) <= lax.broadcasted_iota(jnp.int32, (T, T), 1)
    sums = lax.dot_general(
        jnp.concatenate([dt, sg, dsg], axis=0),
        jnp.where(before, 1.0, 0.0).astype(F32),
        (((1,), (0,)), ((), ())),
        precision=lax.Precision.HIGHEST,
        preferred_element_type=F32,
    )
    cum_dt, cum_sg, cum_dsg = sums[:ROWS], sums[ROWS : 2 * ROWS], sums[2 * ROWS :]
    c = a * cum_dt
    dc = da * cum_dt + a * p_dt * cum_sg
    f0 = a * cum_sg
    f1 = da * cum_sg + a * cum_dsg

    def last(v):
        return jnp.broadcast_to(v[:, T - 1 : T], (ROWS, T))

    g, dg = last(c), last(dc)
    tail = jnp.exp(g - c)
    w = tail * dt
    dw = tail * ((dg - dc) * dt + ddt)
    for k, v in (
        (K_C, c), (K_DC, dc), (K_DT, dt), (K_DDT, ddt), (K_W, w), (K_DW, dw), (K_TAIL, tail), (K_SG, sg),
        (K_DSG, dsg), (K_F0, f0), (K_F1, f1), (K_G, g), (K_DG, dg), (K_F0T, last(f0)), (K_F1T, last(f1)),
        (K_D, d_skip), (K_DD, p_skip),
    ):
        table_ref[k] = v
    cols_ref[...] = jnp.concatenate(
        [c, dc, dt, ddt, jnp.zeros((T - 4 * ROWS, T), F32)], axis=0
    ).T
    total = jnp.zeros((CPD, N), F32)
    d_total = jnp.zeros((CPD, N), F32)
    for b in range(BLK):
        xt = r_ref[b, 0:CPD, :]
        bmat = r_ref[b, CPD : CPD + N, :].astype(BF16)
        parts = split(xt * heads_rows(table_ref, K_W, b)) + split(xt * heads_rows(table_ref, K_DW, b))
        got = mm(jnp.concatenate(parts, axis=0), bmat)
        s = got[0:CPD] + got[CPD : 2 * CPD]
        ds = got[2 * CPD : 3 * CPD] + got[3 * CPD :]
        s_ref[b, 0] = s
        s_ref[b, 1] = ds
        eg = jnp.exp(heads_rows(table_ref, K_G, b))
        d_total = eg * (d_total + heads_rows(table_ref, K_DG, b) * total) + ds
        total = eg * total + s
    write_message(msg_ref, total, d_total, table_ref)


def scan_kernel(reverse, m_ref, o_ref):
    total = jnp.zeros((CPS, N), F32)
    d_total = jnp.zeros((CPS, N), F32)
    for i in range(SEGS - 1, -1, -1) if reverse else range(SEGS):
        o_ref[i, 0:CPS, :] = total
        o_ref[i, CPS : 2 * CPS, :] = d_total
        eg = jnp.exp(m_ref[i, 2 * CPS : 2 * CPS + 1, :])
        dg = m_ref[i, 2 * CPS + 1 : 2 * CPS + 2, :]
        d_total = eg * (d_total + dg * total) + m_ref[i, CPS : 2 * CPS, :]
        total = eg * total + m_ref[i, 0:CPS, :]


def gains(g_ref):
    at = 2 * CPD + T
    halves = CPD // 128
    out = []
    for n in range(2):
        rows = [g_ref[0, at + n * halves + i : at + n * halves + i + 1, :] for i in range(halves)]
        out.append(jnp.concatenate([jnp.broadcast_to(v, (T, 128)).T for v in rows], axis=0))
    return out


def silu(z):
    return z / (1.0 + jnp.exp(-z))


def decays(table, cols, r, scores, causal):
    gap = table[K_C, r : r + 1, :] - cols[:, r : r + 1]
    d_gap = table[K_DC, r : r + 1, :] - cols[:, ROWS + r : ROWS + r + 1]
    return jnp.where(causal, scores * jnp.exp(jnp.where(causal, gap, 0.0)), 0.0), d_gap


def causal_mask():
    return lax.broadcasted_iota(jnp.int32, (T, T), 0) <= lax.broadcasted_iota(jnp.int32, (T, T), 1)


def out_kernel(r_ref, g_ref, h_ref, table_ref, cols_ref, s_ref, y_ref, hb_ref, msg_ref):
    causal = causal_mask()
    gain, dgain = gains(g_ref)
    h = h_ref[:, 0:CPS, :].reshape(CPD, N)
    dh = h_ref[:, CPS : 2 * CPS, :].reshape(CPD, N)
    for b in range(BLK):
        xt = r_ref[b, 0:CPD, :]
        xb = xt.astype(BF16)
        bmat = r_ref[b, CPD : CPD + N, :].astype(BF16)
        cmat = g_ref[b, 2 * CPD : 2 * CPD + T, :].astype(BF16)
        hb_ref[b, 0] = h
        hb_ref[b, 1] = dh
        got = mmt(jnp.concatenate(split(h) + split(dh), axis=0), cmat)
        ch = got[0:CPD] + got[CPD : 2 * CPD]
        dch = got[2 * CPD : 3 * CPD] + got[3 * CPD :]
        scores = mmt(bmat, cmat)
        y_parts, dy_parts = [], []
        for i in range(HPD):
            r = b * HPD + i
            mat, d_gap = decays(table_ref, cols_ref, r, scores, causal)
            dt = cols_ref[:, 2 * ROWS + r : 2 * ROWS + r + 1]
            ddt = cols_ref[:, 3 * ROWS + r : 3 * ROWS + r + 1]
            w = mat * dt
            dw = mat * (d_gap * dt + ddt)
            w_hi, w_lo = split(jnp.concatenate([w, dw], axis=1))
            x_i = xb[i * HD : (i + 1) * HD]
            inner = mm(x_i, w_hi) + mm(x_i, w_lo)
            ec = jnp.exp(table_ref[K_C, r : r + 1, :])
            dc = table_ref[K_DC, r : r + 1, :]
            ch_i, dch_i = ch[i * HD : (i + 1) * HD], dch[i * HD : (i + 1) * HD]
            y_parts.append(inner[:, :T] + ec * ch_i)
            dy_parts.append(inner[:, T:] + ec * (dc * ch_i + dch_i))
        y_nd = jnp.concatenate(y_parts, axis=0)
        dy_nd = jnp.concatenate(dy_parts, axis=0)
        y_ref[0, b] = y_nd
        y_ref[1, b] = dy_nd
        s = silu(g_ref[b, 0:CPD, :])
        cot = g_ref[b, CPD : 2 * CPD, :]
        u = (y_nd + heads_rows(table_ref, K_D, b) * xt) * s
        du = (dy_nd + heads_rows(table_ref, K_DD, b) * xt) * s
        q, dq = gain * cot, dgain * cot
        for n, v in enumerate((u * u, u * q, u * du, du * q + u * dq)):
            row = jnp.sum(v, axis=0, keepdims=True)
            for j in range(BLK):
                msg_ref[j, n * BLK + b : n * BLK + b + 1, :] = row
        eg = jnp.exp(heads_rows(table_ref, K_G, b))
        dh = eg * (dh + heads_rows(table_ref, K_DG, b) * h) + s_ref[b, 1]
        h = eg * h + s_ref[b, 0]


def seed_kernel(r_ref, g_ref, n_ref, table_ref, y_ref, yb_ref, seed_ref, gain_ref, msg_ref):
    gain, dgain = gains(g_ref)
    sums = n_ref[0] + n_ref[1] + n_ref[2] + n_ref[3]
    acc = jnp.zeros((CPD, T), F32)
    adj = jnp.zeros((CPD, N), F32)
    d_adj = jnp.zeros((CPD, N), F32)
    for b in range(BLK - 1, -1, -1):
        xt = r_ref[b, 0:CPD, :]
        cmat = g_ref[b, 2 * CPD : 2 * CPD + T, :].astype(BF16)
        s = silu(g_ref[b, 0:CPD, :])
        cot = g_ref[b, CPD : 2 * CPD, :]
        u = (y_ref[0, b] + heads_rows(table_ref, K_D, b) * xt) * s
        du = (y_ref[1, b] + heads_rows(table_ref, K_DD, b) * xt) * s
        square, m, p, dm = [sums[n * BLK + b : n * BLK + b + 1, :] for n in range(4)]
        mean = square * (1.0 / CH) + EPS
        inv = lax.rsqrt(mean)
        inv = inv * (1.5 - 0.5 * mean * inv * inv)
        cube = inv * inv * inv
        dinv = -cube * p * (1.0 / CH)
        k2 = cube * m * (1.0 / CH)
        k3 = (3.0 * inv * inv * dinv * m + cube * dm) * (1.0 / CH)
        q, dq = gain * cot, dgain * cot
        yb = s * (inv * q - k2 * u)
        dyb = s * (dinv * q + inv * dq - k3 * u - k2 * du)
        yb_ref[0, b] = yb
        yb_ref[1, b] = dyb
        acc = acc + cot * (du * inv + u * dinv)
        ec = jnp.exp(heads_rows(table_ref, K_C, b))
        e0 = ec * yb
        e1 = ec * (heads_rows(table_ref, K_DC, b) * yb + dyb)
        got = mm(jnp.concatenate(split(e0) + split(e1), axis=0), cmat)
        seed = got[0:CPD] + got[CPD : 2 * CPD]
        d_seed = got[2 * CPD : 3 * CPD] + got[3 * CPD :]
        seed_ref[b, 0] = seed
        seed_ref[b, 1] = d_seed
        eg = jnp.exp(heads_rows(table_ref, K_G, b))
        d_adj = eg * (d_adj + heads_rows(table_ref, K_DG, b) * adj) + d_seed
        adj = eg * adj + seed
    for i in range(CPD // 128):
        gain_ref[i : i + 1, :] = jnp.sum(acc[i * 128 : (i + 1) * 128].T, axis=0, keepdims=True)
    write_message(msg_ref, adj, d_adj, table_ref)


def head_sum(v):
    return jnp.sum(v, axis=0, keepdims=True)


def input_kernel(r_ref, g_ref, l_ref, table_ref, cols_ref, y_ref, yb_ref, hb_ref, seed_ref, gain_ref, o_ref, part_ref):
    causal = causal_mask()
    adj = l_ref[:, 0:CPS, :].reshape(CPD, N)
    d_adj = l_ref[:, CPS : 2 * CPS, :].reshape(CPD, N)
    acc_a = [jnp.zeros((1, T), F32) for _ in range(HPD)]
    acc_dt = [jnp.zeros((1, T), F32) for _ in range(HPD)]
    acc_skip = [jnp.zeros((1, T), F32) for _ in range(HPD)]
    for b in range(BLK - 1, -1, -1):
        bmat = r_ref[b, CPD : CPD + N, :].astype(BF16)
        cmat = g_ref[b, 0:T, :].astype(BF16)
        got = mmt(jnp.concatenate(split(adj) + split(d_adj), axis=0), bmat)
        bl = got[0:CPD] + got[CPD : 2 * CPD]
        dbl = got[2 * CPD : 3 * CPD] + got[3 * CPD :]
        scores = mmt(bmat, cmat)
        out_parts = []
        for i in range(HPD):
            r = b * HPD + i
            rows = slice(i * HD, (i + 1) * HD)

            def row(k):
                return table_ref[k, r : r + 1, :]

            mat, d_gap = decays(table_ref, cols_ref, r, scores, causal)
            l_hi, l_lo = split(mat)
            n_hi, n_lo = split(mat * d_gap)
            yb, dyb = yb_ref[0, b, rows, :], yb_ref[1, b, rows, :]
            y_hi, y_lo = split(yb)
            dy_hi, dy_lo = split(dyb)
            got = mmt(jnp.concatenate([y_hi, dy_hi, y_lo, dy_lo], axis=0), l_hi)
            low = mmt(jnp.concatenate([y_hi, dy_hi], axis=0), l_lo)
            both = got[: 2 * HD] + got[2 * HD :] + low
            gap_part = mmt(jnp.concatenate([y_hi, y_lo], axis=0), n_hi)
            gap_part = gap_part[:HD] + gap_part[HD:] + mmt(y_hi, n_lo)
            xt = r_ref[b, rows, :]
            bl_i, dbl_i = bl[rows], dbl[rows]
            tail, dt, ddt, dc, dg = row(K_TAIL), row(K_DT), row(K_DDT), row(K_DC), row(K_DG)
            k = both[:HD] + tail * bl_i
            dk = both[HD:] + gap_part + tail * ((dg - dc) * bl_i + dbl_i)
            out_parts.append(ddt * k + dt * dk + row(K_DD) * yb + row(K_D) * dyb)
            y_nd, dy_nd = y_ref[0, b, rows, :], y_ref[1, b, rows, :]
            xk, dxk = head_sum(xt * k), head_sum(xt * dk)
            e0 = head_sum(yb * y_nd) - dt * xk
            e1 = head_sum(dyb * y_nd + yb * dy_nd) - ddt * xk - dt * dxk
            xbl, dxbl = head_sum(xt * bl_i), head_sum(xt * dbl_i)
            h, dh = hb_ref[b, 0, rows, :], hb_ref[b, 1, rows, :]
            lam, d_lam = adj[rows], d_adj[rows]
            eg = jnp.exp(row(K_G))
            hl = eg * head_sum(lam * h)
            dhl = eg * head_sum(d_lam * h + lam * dh)
            g0 = hl + row(K_W) * xbl
            g1 = dg * hl + dhl + row(K_DW) * xbl + row(K_W) * dxbl
            acc_a[i] = acc_a[i] + dc * e0 + row(K_C) * e1 + dg * g0 + row(K_G) * g1
            acc_dt[i] = (
                acc_dt[i] + row(K_DSG) * xk + row(K_SG) * dxk + row(K_F1) * e0 + row(K_F0) * e1
                + row(K_F1T) * g0 + row(K_F0T) * g1
            )
            acc_skip[i] = acc_skip[i] + head_sum(xt * dyb)
        out = jnp.concatenate(out_parts, axis=0)
        for i in range(CPD // 128):
            o_ref[b, i * 128 : (i + 1) * 128, :] = out[i * 128 : (i + 1) * 128].T
        if b:
            eg = jnp.exp(heads_rows(table_ref, K_G, b))
            d_adj = eg * (d_adj + heads_rows(table_ref, K_DG, b) * adj) + seed_ref[b, 1]
            adj = eg * adj + seed_ref[b, 0]
    for i in range(HPD):
        part_ref[i : i + 1, :] = acc_a[i]
        part_ref[HPD + i : HPD + i + 1, :] = acc_dt[i]
        part_ref[2 * HPD + i : 2 * HPD + i + 1, :] = acc_skip[i]
    part_ref[3 * HPD : 3 * HPD + 2, :] = gain_ref[...]
    part_ref[3 * HPD + 2 :, :] = jnp.zeros((2, T), F32)


def call(kernel, name, outs, in_specs=None):
    def shape(dims):
        return jax.ShapeDtypeStruct(dims, F32)

    many = isinstance(outs, list)
    spec = pl.BlockSpec(memory_space=pltpu.VMEM)

    def run(*args):
        return pl.pallas_call(
            kernel,
            name=name,
            out_shape=[shape(o) for o in outs] if many else shape(outs),
            out_specs=[spec] * len(outs) if many else spec,
            in_specs=in_specs or [spec] * len(args),
            compiler_params=pltpu.CompilerParams(vmem_limit_bytes=VMEM),
        )(*args)

    return run


def per_device(
    ssm_input,
    gate_input,
    b_proj,
    c_proj,
    dt_raw,
    cotangent,
    a_log,
    dt_bias,
    d_skip,
    norm_gain,
    probe_a,
    probe_dt,
    probe_skip,
    probe_gain,
):
    vm, sm = pl.BlockSpec(memory_space=pltpu.VMEM), pl.BlockSpec(memory_space=pltpu.SMEM)

    def exchange(v, axes):
        return lax.all_to_all(v, axes, 0, 0)

    group, segs = "zl", ("y", "zh")
    packed = call(pack_x_kernel, "pack_x", (BLK, X_ROWS, T), [vm] * 3 + [sm] * PARAMS)(
        ssm_input, b_proj, dt_raw.T, a_log, dt_bias, d_skip, probe_a, probe_dt, probe_skip
    )
    r = exchange(packed, group)
    packed_g = call(pack_g_kernel, "pack_g", (BLK, G_ROWS, T))(
        gate_input, cotangent, c_proj, norm_gain.reshape(8, 128), probe_gain.reshape(8, 128)
    )
    g = exchange(packed_g, group)
    table, cols, s, msg = call(
        state_kernel,
        "state",
        [(TABLE, ROWS, T), (T, T), (BLK, 2, CPD, N), (SEGS, M_ROWS, N)],
    )(r)
    before = call(functools.partial(scan_kernel, False), "scan_up", (SEGS, 2 * CPS, N))(exchange(msg, segs))
    h_in = exchange(before, segs)
    y, h_blocks, norms = call(
        out_kernel, "mix", [(2, BLK, CPD, T), (BLK, 2, CPD, N), (BLK, 4 * BLK, T)]
    )(r, g, h_in, table, cols, s)
    norms = exchange(norms, group)
    y_bar, seeds, d_gain, msg = call(
        seed_kernel,
        "seeds",
        [(2, BLK, CPD, T), (BLK, 2, CPD, N), (2, 128), (SEGS, M_ROWS, N)],
    )(r, g, norms, table, y)
    after = call(functools.partial(scan_kernel, True), "scan_down", (SEGS, 2 * CPS, N))(exchange(msg, segs))
    adj = exchange(after, segs)
    c_all = g[:, 2 * CPD : 2 * CPD + T, :]
    out, part = call(input_kernel, "input_grad", [(BLK, CPD, 128), (4 * HPD, T)])(
        r, c_all, adj, table, cols, y, y_bar, h_blocks, seeds, d_gain
    )
    out = exchange(out, group).reshape(CH // 128, T, 128)
    hvp_input = jnp.transpose(out, (1, 0, 2)).reshape(T, CH)

    devices = lax.axis_size("dp")
    part = jnp.sum(exchange(jnp.broadcast_to(part[None], (devices,) + part.shape), "dp"), axis=0)
    whole = SEGS * BLK
    part = exchange(jnp.broadcast_to(part[None], (whole,) + part.shape), ("y", "zh", "zl"))
    part = jnp.sum(part.reshape(SEGS, BLK, 4 * HPD, T), axis=0)
    factor = 1.0 / math.sqrt(T * devices * whole)
    heads = jnp.sum(part[:, : 3 * HPD, :], axis=2).reshape(BLK, 3, HPD) * factor
    hvp_gain = part[:, 3 * HPD : 3 * HPD + 2, :].reshape(CH) * factor
    return (
        hvp_input,
        heads[:, 0].reshape(HEADS),
        heads[:, 1].reshape(HEADS),
        heads[:, 2].reshape(HEADS),
        hvp_gain,
    )


def solution(mesh):
    fine = Mesh(mesh.devices.reshape(mesh.devices.shape[0], 4, 2, 4), ("dp", "y", "zh", "zl"))
    tokens = P(("dp", "y", "zh", "zl"), None)
    return jax.shard_map(
        per_device,
        mesh=fine,
        in_specs=(tokens,) * 6 + (P(),) * 8,
        out_specs=(tokens, P(), P(), P(), P()),
        check_vma=False,
    )
```

```python
import functools
import math

import jax
import jax.numpy as jnp
from jax import lax
from jax.experimental import pallas as pl
from jax.experimental.pallas import tpu as pltpu
from jax.sharding import Mesh, PartitionSpec as P

F32, BF16 = jnp.float32, jnp.bfloat16
EPS = 1e-05
T = 128
N = 128
HD = 64
HEADS = 16
CH = 1024
BLK = 4
HPD = HEADS // BLK
CPD = HPD * HD
ROWS = BLK * HPD
SEGS = 8
CPS = CPD // SEGS
PARAMS = 6
NEAR = 32
FAR = 16
FIRST = (1,)
EARLY = (2, 3)
X_ROWS = CPD + N + HPD + 4
G_ROWS = 2 * CPD + T + 8
M_ROWS = 2 * CPS + 8
VMEM = 16 * 1024 * 1024

(K_C, K_DC, K_DT, K_DDT, K_W, K_DW, K_TAIL, K_SG, K_DSG, K_F0, K_F1, K_G, K_DG, K_F0T, K_F1T, K_D, K_DD) = range(17)
TABLE = 17


def split(a):
    hi = a.astype(BF16)
    return hi, (a - hi.astype(F32)).astype(BF16)


def mm(a, b):
    return lax.dot_general(a, b, (((1,), (0,)), ((), ())), preferred_element_type=F32)


def mmt(a, b):
    return lax.dot_general(a, b, (((1,), (1,)), ((), ())), preferred_element_type=F32)


def heads_rows(table, k, b):
    return jnp.concatenate(
        [jnp.broadcast_to(table[k, b * HPD + h : b * HPD + h + 1, :], (HD, T)) for h in range(HPD)], axis=0
    )


def pack_x_kernel(x_ref, b_ref, dt_ref, o_ref):
    for j in range(BLK):
        for i in range(CPD // 128):
            lo = j * CPD + i * 128
            o_ref[j, i * 128 : (i + 1) * 128, :] = x_ref[:, lo : lo + 128].astype(F32).T
        o_ref[j, CPD : CPD + N, :] = b_ref[...].astype(F32)
        at = CPD + N
        o_ref[j, at : at + HPD, :] = dt_ref[j * HPD : (j + 1) * HPD, :]
        at += HPD
        o_ref[j, at:X_ROWS, :] = jnp.zeros((X_ROWS - at, T), F32)


def pack_g_kernel(zl_ref, z_ref, cot_ref, c_ref, gain_ref, dgain_ref, after_ref, *o_refs):
    del after_ref
    halves = CPD // 128
    for d, o_ref in enumerate(o_refs):
        j = lax.rem(zl_ref[0] + d, BLK)
        for n, ref in enumerate((z_ref, cot_ref)):
            for i in range(halves):
                lo = pl.multiple_of(j * CPD + i * 128, 128)
                at = n * CPD + i * 128
                o_ref[at : at + 128, :] = ref[:, pl.ds(lo, 128)].astype(F32).T
        o_ref[2 * CPD : 2 * CPD + T, :] = c_ref[...].astype(F32)
        at = 2 * CPD + T
        for i in range(halves):
            o_ref[at + i : at + i + 1, :] = gain_ref[pl.ds(j * halves + i, 1), :]
            o_ref[at + halves + i : at + halves + i + 1, :] = dgain_ref[pl.ds(j * halves + i, 1), :]
        o_ref[at + 2 * halves : at + 8, :] = jnp.zeros((8 - 2 * halves, 128), F32)


def write_message(msg_ref, total, d_total):
    for j in range(SEGS):
        msg_ref[j, 0:CPS, :] = total[j * CPS : (j + 1) * CPS]
        msg_ref[j, CPS : 2 * CPS, :] = d_total[j * CPS : (j + 1) * CPS]


def write_decay(msg_ref, table):
    for j in range(SEGS):
        h = j * CPS // HD
        g, dg = None, None
        for b in range(BLK):
            r = b * HPD + h
            g_b, dg_b = table[K_G, r : r + 1, :], table[K_DG, r : r + 1, :]
            g, dg = (g_b, dg_b) if g is None else (g + g_b, dg + dg_b)
        msg_ref[j, 2 * CPS : 2 * CPS + 1, :] = g
        msg_ref[j, 2 * CPS + 1 : 2 * CPS + 2, :] = dg
        msg_ref[j, 2 * CPS + 2 : M_ROWS, :] = jnp.zeros((M_ROWS - 2 * CPS - 2, T), F32)


def state_kernel(zl_ref, *rest):
    prm, r_ref = rest[:PARAMS], rest[PARAMS]
    table_ref, cols_ref, s_ref, msg_ref = rest[-4:]
    at = CPD + N
    raw = jnp.concatenate([r_ref[b, at : at + HPD, :] for b in range(BLK)], axis=0)

    def head_values(ref):
        return jnp.concatenate([jnp.full((1, T), ref[zl_ref[0] * HPD + h], F32) for h in range(HPD)] * BLK, axis=0)

    a_log, dt_bias, d_skip, p_a, p_dt, p_skip = [head_values(ref) for ref in prm]
    pre = raw + dt_bias
    dt = jnp.maximum(pre, 0.0) + jnp.log1p(jnp.exp(-jnp.abs(pre)))
    sg = 1.0 / (1.0 + jnp.exp(-pre))
    dsg = sg * (1.0 - sg) * p_dt
    ddt = sg * p_dt
    a = -jnp.exp(a_log)
    da = a * p_a
    before = lax.broadcasted_iota(jnp.int32, (T, T), 0) <= lax.broadcasted_iota(jnp.int32, (T, T), 1)
    sums = lax.dot_general(
        jnp.concatenate([dt, sg, dsg], axis=0),
        jnp.where(before, 1.0, 0.0).astype(F32),
        (((1,), (0,)), ((), ())),
        precision=lax.Precision.HIGHEST,
        preferred_element_type=F32,
    )
    cum_dt, cum_sg, cum_dsg = sums[:ROWS], sums[ROWS : 2 * ROWS], sums[2 * ROWS :]
    c = a * cum_dt
    dc = da * cum_dt + a * p_dt * cum_sg
    f0 = a * cum_sg
    f1 = da * cum_sg + a * cum_dsg

    def last(v):
        return jnp.broadcast_to(v[:, T - 1 : T], (ROWS, T))

    g, dg = last(c), last(dc)
    tail = jnp.exp(g - c)
    w = tail * dt
    dw = tail * ((dg - dc) * dt + ddt)
    for k, v in (
        (K_C, c), (K_DC, dc), (K_DT, dt), (K_DDT, ddt), (K_W, w), (K_DW, dw), (K_TAIL, tail), (K_SG, sg),
        (K_DSG, dsg), (K_F0, f0), (K_F1, f1), (K_G, g), (K_DG, dg), (K_F0T, last(f0)), (K_F1T, last(f1)),
        (K_D, d_skip), (K_DD, p_skip),
    ):
        table_ref[k] = v
    cols_ref[...] = jnp.concatenate(
        [c, dc, dt, ddt, jnp.zeros((T - 4 * ROWS, T), F32)], axis=0
    ).T
    total = jnp.zeros((CPD, N), F32)
    d_total = jnp.zeros((CPD, N), F32)
    for b in range(BLK):
        xt = r_ref[b, 0:CPD, :]
        bmat = r_ref[b, CPD : CPD + N, :].astype(BF16)
        parts = split(xt * heads_rows(table_ref, K_W, b)) + split(xt * heads_rows(table_ref, K_DW, b))
        got = mm(jnp.concatenate(parts, axis=0), bmat)
        s = got[0:CPD] + got[CPD : 2 * CPD]
        ds = got[2 * CPD : 3 * CPD] + got[3 * CPD :]
        s_ref[b, 0] = s
        s_ref[b, 1] = ds
        eg = jnp.exp(heads_rows(table_ref, K_G, b))
        d_total = eg * (d_total + heads_rows(table_ref, K_DG, b) * total) + ds
        total = eg * total + s
    write_message(msg_ref, total, d_total)
    write_decay(msg_ref, table_ref)


def scan_kernel(reverse, decay_ref, m_ref, o_ref):
    total = jnp.zeros((CPS, N), F32)
    d_total = jnp.zeros((CPS, N), F32)
    for i in range(SEGS - 1, -1, -1) if reverse else range(SEGS):
        o_ref[i, 0:CPS, :] = total
        o_ref[i, CPS : 2 * CPS, :] = d_total
        eg = jnp.exp(decay_ref[i, 2 * CPS : 2 * CPS + 1, :])
        dg = decay_ref[i, 2 * CPS + 1 : 2 * CPS + 2, :]
        d_total = eg * (d_total + dg * total) + m_ref[i, CPS : 2 * CPS, :]
        total = eg * total + m_ref[i, 0:CPS, :]


def scan_up_kernel(m_ref, *rest):
    scan_kernel(False, m_ref, m_ref, rest[-1])


def gains(g_ref):
    at = 2 * CPD + T
    halves = CPD // 128
    out = []
    for n in range(2):
        rows = [g_ref[0, at + n * halves + i : at + n * halves + i + 1, :] for i in range(halves)]
        out.append(jnp.concatenate([jnp.broadcast_to(v, (T, 128)).T for v in rows], axis=0))
    return out


def silu(z):
    return z / (1.0 + jnp.exp(-z))


def decays(table, cols, r, scores, causal):
    gap = table[K_C, r : r + 1, :] - cols[:, r : r + 1]
    d_gap = table[K_DC, r : r + 1, :] - cols[:, ROWS + r : ROWS + r + 1]
    return jnp.where(causal, scores * jnp.exp(jnp.where(causal, gap, 0.0)), 0.0), d_gap


def causal_mask():
    return lax.broadcasted_iota(jnp.int32, (T, T), 0) <= lax.broadcasted_iota(jnp.int32, (T, T), 1)


def out_kernel(
    zl_ref, r_ref, g0, g1, g2, g3, h_ref, table_ref, cols_ref, s_ref, g_ref, y_ref, hb_ref, msg_ref, sems
):
    copies = []
    for d, src in enumerate((g0, g1, g2, g3)):
        b = lax.rem(zl_ref[0] + BLK - d, BLK)
        copies.append(pltpu.make_async_copy(src, g_ref.at[b], sems.at[d]))
        copies[-1].start()
    for copy in copies:
        copy.wait()
    causal = causal_mask()
    gain, dgain = gains(g_ref)
    h = h_ref[:, 0:CPS, :].reshape(CPD, N)
    dh = h_ref[:, CPS : 2 * CPS, :].reshape(CPD, N)
    for b in range(BLK):
        xt = r_ref[b, 0:CPD, :]
        xb = xt.astype(BF16)
        bmat = r_ref[b, CPD : CPD + N, :].astype(BF16)
        cmat = g_ref[b, 2 * CPD : 2 * CPD + T, :].astype(BF16)
        hb_ref[b, 0] = h
        hb_ref[b, 1] = dh
        got = mmt(jnp.concatenate(split(h) + split(dh), axis=0), cmat)
        ch = got[0:CPD] + got[CPD : 2 * CPD]
        dch = got[2 * CPD : 3 * CPD] + got[3 * CPD :]
        scores = mmt(bmat, cmat)
        y_parts, dy_parts = [], []
        for i in range(HPD):
            r = b * HPD + i
            mat, d_gap = decays(table_ref, cols_ref, r, scores, causal)
            dt = cols_ref[:, 2 * ROWS + r : 2 * ROWS + r + 1]
            ddt = cols_ref[:, 3 * ROWS + r : 3 * ROWS + r + 1]
            w = mat * dt
            dw = mat * (d_gap * dt + ddt)
            w_hi, w_lo = split(jnp.concatenate([w, dw], axis=1))
            x_i = xb[i * HD : (i + 1) * HD]
            inner = mm(x_i, w_hi) + mm(x_i, w_lo)
            ec = jnp.exp(table_ref[K_C, r : r + 1, :])
            dc = table_ref[K_DC, r : r + 1, :]
            ch_i, dch_i = ch[i * HD : (i + 1) * HD], dch[i * HD : (i + 1) * HD]
            y_parts.append(inner[:, :T] + ec * ch_i)
            dy_parts.append(inner[:, T:] + ec * (dc * ch_i + dch_i))
        y_nd = jnp.concatenate(y_parts, axis=0)
        dy_nd = jnp.concatenate(dy_parts, axis=0)
        y_ref[0, b] = y_nd
        y_ref[1, b] = dy_nd
        s = silu(g_ref[b, 0:CPD, :])
        cot = g_ref[b, CPD : 2 * CPD, :]
        u = (y_nd + heads_rows(table_ref, K_D, b) * xt) * s
        du = (dy_nd + heads_rows(table_ref, K_DD, b) * xt) * s
        q, dq = gain * cot, dgain * cot
        for n, v in enumerate((u * u, u * q, u * du, du * q + u * dq)):
            row = jnp.sum(v, axis=0, keepdims=True)
            for j in range(BLK):
                msg_ref[j, n * BLK + b : n * BLK + b + 1, :] = row
        eg = jnp.exp(heads_rows(table_ref, K_G, b))
        dh = eg * (dh + heads_rows(table_ref, K_DG, b) * h) + s_ref[b, 1]
        h = eg * h + s_ref[b, 0]


def seed_kernel(r_ref, g_ref, n_ref, table_ref, y_ref, yb_ref, seed_ref, gain_ref, msg_ref):
    gain, dgain = gains(g_ref)
    sums = n_ref[0] + n_ref[1] + n_ref[2] + n_ref[3]
    acc = jnp.zeros((CPD, T), F32)
    adj = jnp.zeros((CPD, N), F32)
    d_adj = jnp.zeros((CPD, N), F32)
    for b in range(BLK - 1, -1, -1):
        xt = r_ref[b, 0:CPD, :]
        cmat = g_ref[b, 2 * CPD : 2 * CPD + T, :].astype(BF16)
        s = silu(g_ref[b, 0:CPD, :])
        cot = g_ref[b, CPD : 2 * CPD, :]
        u = (y_ref[0, b] + heads_rows(table_ref, K_D, b) * xt) * s
        du = (y_ref[1, b] + heads_rows(table_ref, K_DD, b) * xt) * s
        square, m, p, dm = [sums[n * BLK + b : n * BLK + b + 1, :] for n in range(4)]
        mean = square * (1.0 / CH) + EPS
        inv = lax.rsqrt(mean)
        inv = inv * (1.5 - 0.5 * mean * inv * inv)
        cube = inv * inv * inv
        dinv = -cube * p * (1.0 / CH)
        k2 = cube * m * (1.0 / CH)
        k3 = (3.0 * inv * inv * dinv * m + cube * dm) * (1.0 / CH)
        q, dq = gain * cot, dgain * cot
        yb = s * (inv * q - k2 * u)
        dyb = s * (dinv * q + inv * dq - k3 * u - k2 * du)
        yb_ref[0, b] = yb
        yb_ref[1, b] = dyb
        acc = acc + cot * (du * inv + u * dinv)
        ec = jnp.exp(heads_rows(table_ref, K_C, b))
        e0 = ec * yb
        e1 = ec * (heads_rows(table_ref, K_DC, b) * yb + dyb)
        got = mm(jnp.concatenate(split(e0) + split(e1), axis=0), cmat)
        seed = got[0:CPD] + got[CPD : 2 * CPD]
        d_seed = got[2 * CPD : 3 * CPD] + got[3 * CPD :]
        seed_ref[b, 0] = seed
        seed_ref[b, 1] = d_seed
        eg = jnp.exp(heads_rows(table_ref, K_G, b))
        d_adj = eg * (d_adj + heads_rows(table_ref, K_DG, b) * adj) + d_seed
        adj = eg * adj + seed
    for i in range(CPD // 128):
        gain_ref[i : i + 1, :] = jnp.sum(acc[i * 128 : (i + 1) * 128].T, axis=0, keepdims=True)
    write_message(msg_ref, adj, d_adj)


def head_sum(v):
    return jnp.sum(v, axis=0, keepdims=True)


def input_kernel(
    zl_ref, r_ref, g_ref, l_ref, table_ref, cols_ref, y_ref, yb_ref, hb_ref, seed_ref, gain_ref, *rest
):
    o_refs, part_ref, o_ref, sems = rest[:BLK], rest[BLK], rest[BLK + 1], rest[BLK + 2]
    causal = causal_mask()
    adj = l_ref[:, 0:CPS, :].reshape(CPD, N)
    d_adj = l_ref[:, CPS : 2 * CPS, :].reshape(CPD, N)
    acc_a = [jnp.zeros((1, T), F32) for _ in range(HPD)]
    acc_dt = [jnp.zeros((1, T), F32) for _ in range(HPD)]
    acc_skip = [jnp.zeros((1, T), F32) for _ in range(HPD)]
    for b in range(BLK - 1, -1, -1):
        bmat = r_ref[b, CPD : CPD + N, :].astype(BF16)
        cmat = g_ref[b, 2 * CPD : 2 * CPD + T, :].astype(BF16)
        got = mmt(jnp.concatenate(split(adj) + split(d_adj), axis=0), bmat)
        bl = got[0:CPD] + got[CPD : 2 * CPD]
        dbl = got[2 * CPD : 3 * CPD] + got[3 * CPD :]
        scores = mmt(bmat, cmat)
        out_parts = []
        for i in range(HPD):
            r = b * HPD + i
            rows = slice(i * HD, (i + 1) * HD)

            def row(k):
                return table_ref[k, r : r + 1, :]

            mat, d_gap = decays(table_ref, cols_ref, r, scores, causal)
            l_hi, l_lo = split(mat)
            n_hi, n_lo = split(mat * d_gap)
            yb, dyb = yb_ref[0, b, rows, :], yb_ref[1, b, rows, :]
            y_hi, y_lo = split(yb)
            dy_hi, dy_lo = split(dyb)
            got = mmt(jnp.concatenate([y_hi, dy_hi, y_lo, dy_lo], axis=0), l_hi)
            low = mmt(jnp.concatenate([y_hi, dy_hi], axis=0), l_lo)
            both = got[: 2 * HD] + got[2 * HD :] + low
            gap_part = mmt(jnp.concatenate([y_hi, y_lo], axis=0), n_hi)
            gap_part = gap_part[:HD] + gap_part[HD:] + mmt(y_hi, n_lo)
            xt = r_ref[b, rows, :]
            bl_i, dbl_i = bl[rows], dbl[rows]
            tail, dt, ddt, dc, dg = row(K_TAIL), row(K_DT), row(K_DDT), row(K_DC), row(K_DG)
            k = both[:HD] + tail * bl_i
            dk = both[HD:] + gap_part + tail * ((dg - dc) * bl_i + dbl_i)
            out_parts.append(ddt * k + dt * dk + row(K_DD) * yb + row(K_D) * dyb)
            y_nd, dy_nd = y_ref[0, b, rows, :], y_ref[1, b, rows, :]
            xk, dxk = head_sum(xt * k), head_sum(xt * dk)
            e0 = head_sum(yb * y_nd) - dt * xk
            e1 = head_sum(dyb * y_nd + yb * dy_nd) - ddt * xk - dt * dxk
            xbl, dxbl = head_sum(xt * bl_i), head_sum(xt * dbl_i)
            h, dh = hb_ref[b, 0, rows, :], hb_ref[b, 1, rows, :]
            lam, d_lam = adj[rows], d_adj[rows]
            eg = jnp.exp(row(K_G))
            hl = eg * head_sum(lam * h)
            dhl = eg * head_sum(d_lam * h + lam * dh)
            g0 = hl + row(K_W) * xbl
            g1 = dg * hl + dhl + row(K_DW) * xbl + row(K_W) * dxbl
            acc_a[i] = acc_a[i] + dc * e0 + row(K_C) * e1 + dg * g0 + row(K_G) * g1
            acc_dt[i] = (
                acc_dt[i] + row(K_DSG) * xk + row(K_SG) * dxk + row(K_F1) * e0 + row(K_F0) * e1
                + row(K_F1T) * g0 + row(K_F0T) * g1
            )
            acc_skip[i] = acc_skip[i] + head_sum(xt * dyb)
        out = jnp.concatenate(out_parts, axis=0)
        for i in range(CPD // 128):
            o_ref[b, i * 128 : (i + 1) * 128, :] = out[i * 128 : (i + 1) * 128].T
        if b:
            eg = jnp.exp(heads_rows(table_ref, K_G, b))
            d_adj = eg * (d_adj + heads_rows(table_ref, K_DG, b) * adj) + seed_ref[b, 1]
            adj = eg * adj + seed_ref[b, 0]
    part = jnp.concatenate(acc_a + acc_dt + acc_skip + [gain_ref[...], jnp.zeros((2, T), F32)], axis=0)
    copies = []
    for d in range(BLK):
        copies.append(pltpu.make_async_copy(o_ref.at[lax.rem(zl_ref[0] + d, BLK)], o_refs[d], sems.at[d]))
        copies[-1].start()
    for i in range(NEAR):
        part_ref[i] = part
    for copy in copies:
        copy.wait()


def place_kernel(zl_ref, i0, i1, i2, i3, o_ref, sems):
    copies = []
    for d, src in enumerate((i0, i1, i2, i3)):
        j = lax.rem(zl_ref[0] + BLK - d, BLK)
        for i in range(CPD // 128):
            lo = pl.multiple_of(j * CPD + i * 128, 128)
            copies.append(
                pltpu.make_async_copy(
                    src.at[pl.ds(i * 128, 128), :], o_ref.at[:, pl.ds(lo, 128)], sems.at[len(copies)]
                )
            )
            copies[-1].start()
    for copy in copies:
        copy.wait()


def sum_kernel(m_ref, o_ref):
    total = m_ref[0]
    for i in range(1, NEAR):
        total = total + m_ref[i]
    for i in range(FAR):
        o_ref[i] = total


def finish_kernel(factor, m_ref, a_ref, dt_ref, skip_ref, gain_ref):
    outs = (a_ref, dt_ref, skip_ref)
    rows = [[] for _ in outs]
    for j in range(BLK):
        total = m_ref[j]
        for i in range(1, FAR // BLK):
            total = total + m_ref[i * BLK + j]
        total = total * factor
        for n in range(len(outs)):
            rows[n].append(total[n * HPD : (n + 1) * HPD, :])
        gain_ref[2 * j : 2 * j + 2, :] = total[3 * HPD : 3 * HPD + 2, :]
    for n, ref in enumerate(outs):
        ref[...] = jnp.sum(jnp.concatenate(rows[n], axis=0).T, axis=0, keepdims=True)


def call(kernel, name, outs, in_specs=None, scratch=(), out_specs=None):
    def shape(dims):
        return jax.ShapeDtypeStruct(dims, F32)

    many = isinstance(outs, list)
    spec = pl.BlockSpec(memory_space=pltpu.VMEM)

    def run(*args):
        return pl.pallas_call(
            kernel,
            name=name,
            out_shape=[shape(o) for o in outs] if many else shape(outs),
            out_specs=out_specs or ([spec] * len(outs) if many else spec),
            in_specs=in_specs or [spec] * len(args),
            scratch_shapes=list(scratch),
            compiler_params=pltpu.CompilerParams(vmem_limit_bytes=VMEM),
        )(*args)

    return run


def per_device(
    ssm_input,
    gate_input,
    b_proj,
    c_proj,
    dt_raw,
    cotangent,
    a_log,
    dt_bias,
    d_skip,
    norm_gain,
    probe_a,
    probe_dt,
    probe_skip,
    probe_gain,
):
    vm, sm, hbm = [pl.BlockSpec(memory_space=m) for m in (pltpu.VMEM, pltpu.SMEM, pltpu.HBM)]

    def exchange(v, axes):
        return lax.all_to_all(v, axes, 0, 0)

    group, segs = "zl", ("y", "zh")

    def shift(v, d):
        return lax.ppermute(v, group, [(i, (i + d) % BLK) for i in range(BLK)])

    zl = lax.axis_index(group).reshape(1)
    packed = call(pack_x_kernel, "pack_x", (BLK, X_ROWS, T))(ssm_input, b_proj, dt_raw.T)
    r = exchange(packed, group)
    parts = call(pack_g_kernel, "pack_g", [(G_ROWS, T)] * BLK, [sm] + [vm] * 5 + [hbm])(
        zl, gate_input, cotangent, c_proj, norm_gain.reshape(8, 128), probe_gain.reshape(8, 128), norm_gain
    )
    parts = [shift(v, d) if d else v for d, v in enumerate(parts)]
    table, cols, s, msg = call(
        state_kernel,
        "state",
        [(TABLE, ROWS, T), (T, T), (BLK, 2, CPD, N), (SEGS, M_ROWS, N)],
        [sm] * (1 + PARAMS) + [vm] + [hbm] * len(FIRST),
    )(zl, a_log, dt_bias, d_skip, probe_a, probe_dt, probe_skip, r, *[parts[d] for d in FIRST])
    decay = exchange(msg, segs)
    early = [parts[d] for d in EARLY]
    before = call(scan_up_kernel, "scan_up", (SEGS, 2 * CPS, N), [vm] + [hbm] * len(early))(decay, *early)
    h_in = exchange(before, segs)
    g, y, h_blocks, norms = call(
        out_kernel,
        "mix",
        [(BLK, G_ROWS, T), (2, BLK, CPD, T), (BLK, 2, CPD, N), (BLK, 4 * BLK, T)],
        [sm, vm] + [hbm] * BLK + [vm] * 4,
        [pltpu.SemaphoreType.DMA((BLK,))],
    )(zl, r, *parts, h_in, table, cols, s)
    norms = exchange(norms, group)
    y_bar, seeds, d_gain, msg = call(
        seed_kernel,
        "seeds",
        [(2, BLK, CPD, T), (BLK, 2, CPD, N), (2, 128), (SEGS, 2 * CPS, N)],
    )(r, g, norms, table, y)
    after = call(functools.partial(scan_kernel, True), "scan_down", (SEGS, 2 * CPS, N))(
        decay, exchange(msg, segs)
    )
    adj = exchange(after, segs)
    *outs, part = call(
        input_kernel,
        "input_grad",
        [(CPD, 128)] * BLK + [(NEAR, 4 * HPD, T)],
        [sm] + [vm] * 10,
        [pltpu.VMEM((BLK, CPD, 128), F32), pltpu.SemaphoreType.DMA((BLK,))],
        [hbm] * BLK + [vm],
    )(zl, r, g, adj, table, cols, y, y_bar, h_blocks, seeds, d_gain)
    outs = [shift(v, d) if d else v for d, v in enumerate(outs)]
    part = call(sum_kernel, "near_sum", (FAR, 4 * HPD, T))(exchange(part, ("x", "core", "y")))
    hvp_input = call(
        place_kernel,
        "place",
        (T, CH),
        [sm] + [hbm] * BLK,
        [pltpu.SemaphoreType.DMA((CH // 128,))],
        hbm,
    )(zl, *outs)
    factor = 1.0 / math.sqrt(T * NEAR * FAR)
    hvp_a, hvp_dt, hvp_skip, hvp_gain = call(
        functools.partial(finish_kernel, factor), "finish", [(1, HEADS)] * 3 + [(8, 128)]
    )(exchange(part, ("zhi", "zh", "zl")))
    return (
        hvp_input,
        hvp_a.reshape(HEADS),
        hvp_dt.reshape(HEADS),
        hvp_skip.reshape(HEADS),
        hvp_gain.reshape(CH),
    )


def solution(mesh):
    axes = ("zhi", "x", "core", "y", "zh", "zl")
    fine = Mesh(mesh.devices.reshape(2, 4, 2, 4, 2, 4), axes)
    tokens = P(axes, None)
    return jax.shard_map(
        per_device,
        mesh=fine,
        in_specs=(tokens,) * 6 + (P(),) * 8,
        out_specs=(tokens, P(), P(), P(), P()),
        check_vma=False,
    )
```

```python
import functools
import math

import jax
import jax.numpy as jnp
from jax import lax
from jax.experimental import pallas as pl
from jax.experimental.pallas import tpu as pltpu
from jax.sharding import Mesh, PartitionSpec as P

F32, BF16 = jnp.float32, jnp.bfloat16
EPS = 1e-05
T = 128
N = 128
HD = 64
HEADS = 16
CH = 1024
BLK = 4
HPD = HEADS // BLK
CPD = HPD * HD
ROWS = BLK * HPD
SEGS = 8
CPS = CPD // SEGS
PARAMS = 6
NEAR = 32
FAR = 16
FIRST = (1,)
EARLY = (2,)
BACK = (2,)
X_ROWS = CPD + N + HPD + 4
G_ROWS = 2 * CPD + T
M_ROWS = 2 * CPS + 8
VMEM = 16 * 1024 * 1024

(K_C, K_DC, K_DT, K_DDT, K_W, K_DW, K_TAIL, K_SG, K_DSG, K_F0, K_F1, K_G, K_DG, K_F0T, K_F1T, K_D, K_DD) = range(17)
TABLE = 17


def split(a):
    hi = a.astype(BF16)
    return hi, (a - hi.astype(F32)).astype(BF16)


def mm(a, b):
    return lax.dot_general(a, b, (((1,), (0,)), ((), ())), preferred_element_type=F32)


def mmt(a, b):
    return lax.dot_general(a, b, (((1,), (1,)), ((), ())), preferred_element_type=F32)


def heads_rows(table, k, b):
    return jnp.concatenate(
        [jnp.broadcast_to(table[k, b * HPD + h : b * HPD + h + 1, :], (HD, T)) for h in range(HPD)], axis=0
    )


def pack_x_kernel(x_hbm, b_hbm, dt_hbm, o_ref, x_ref, b_ref, dt_ref, sems):
    pairs = ((x_hbm, x_ref), (b_hbm, b_ref), (dt_hbm, dt_ref))
    copies = [pltpu.make_async_copy(src, dst, sems.at[n]) for n, (src, dst) in enumerate(pairs)]
    for copy in copies:
        copy.start()
    for copy in copies:
        copy.wait()
    for j in range(BLK):
        for i in range(CPD // 128):
            lo = j * CPD + i * 128
            o_ref[j, i * 128 : (i + 1) * 128, :] = x_ref[:, lo : lo + 128].astype(F32).T
        o_ref[j, CPD : CPD + N, :] = b_ref[...].astype(F32)
        at = CPD + N
        o_ref[j, at : at + HPD, :] = dt_ref[j * HPD : (j + 1) * HPD, :]
        at += HPD
        o_ref[j, at:X_ROWS, :] = jnp.zeros((X_ROWS - at, T), F32)


def pack_g_kernel(zl_ref, z_ref, cot_ref, c_ref, *rest):
    o_refs, made, sems = rest[:BLK], rest[BLK : 2 * BLK], rest[2 * BLK]
    copies = [pltpu.make_async_copy(made[d], o_refs[d], sems.at[d]) for d in range(BLK)]
    for d in (*range(1, BLK), 0):
        o_ref = made[d]
        j = lax.rem(zl_ref[0] + d, BLK)
        for n, ref in enumerate((z_ref, cot_ref)):
            for i in range(CPD // 128):
                lo = pl.multiple_of(j * CPD + i * 128, 128)
                at = n * CPD + i * 128
                o_ref[at : at + 128, :] = ref[:, pl.ds(lo, 128)].astype(F32).T
        o_ref[2 * CPD : 2 * CPD + T, :] = c_ref[...].astype(F32)
        copies[d].start()
    for copy in copies:
        copy.wait()


def write_message(msg_ref, total, d_total):
    for j in range(SEGS):
        msg_ref[j, 0:CPS, :] = total[j * CPS : (j + 1) * CPS]
        msg_ref[j, CPS : 2 * CPS, :] = d_total[j * CPS : (j + 1) * CPS]


def write_decay(msg_ref, table):
    for j in range(SEGS):
        h = j * CPS // HD
        g, dg = None, None
        for b in range(BLK):
            r = b * HPD + h
            g_b, dg_b = table[K_G, r : r + 1, :], table[K_DG, r : r + 1, :]
            g, dg = (g_b, dg_b) if g is None else (g + g_b, dg + dg_b)
        msg_ref[j, 2 * CPS : 2 * CPS + 1, :] = g
        msg_ref[j, 2 * CPS + 1 : 2 * CPS + 2, :] = dg
        msg_ref[j, 2 * CPS + 2 : M_ROWS, :] = jnp.zeros((M_ROWS - 2 * CPS - 2, T), F32)


def state_kernel(prm_ref, r_ref, *rest):
    table_ref, s_ref, msg_ref = rest[-3:]
    at = CPD + N
    raw = jnp.concatenate([r_ref[b, at : at + HPD, :] for b in range(BLK)], axis=0)

    a_log, dt_bias, d_skip, p_a, p_dt, p_skip = [
        jnp.concatenate([prm_ref[k * HPD : (k + 1) * HPD, :]] * BLK, axis=0) for k in range(PARAMS)
    ]
    pre = raw + dt_bias
    dt = jnp.maximum(pre, 0.0) + jnp.log1p(jnp.exp(-jnp.abs(pre)))
    sg = 1.0 / (1.0 + jnp.exp(-pre))
    dsg = sg * (1.0 - sg) * p_dt
    ddt = sg * p_dt
    a = -jnp.exp(a_log)
    da = a * p_a
    before = lax.broadcasted_iota(jnp.int32, (T, T), 0) <= lax.broadcasted_iota(jnp.int32, (T, T), 1)
    sums = lax.dot_general(
        jnp.concatenate([dt, sg, dsg], axis=0),
        jnp.where(before, 1.0, 0.0).astype(F32),
        (((1,), (0,)), ((), ())),
        precision=lax.Precision.HIGHEST,
        preferred_element_type=F32,
    )
    cum_dt, cum_sg, cum_dsg = sums[:ROWS], sums[ROWS : 2 * ROWS], sums[2 * ROWS :]
    c = a * cum_dt
    dc = da * cum_dt + a * p_dt * cum_sg
    f0 = a * cum_sg
    f1 = da * cum_sg + a * cum_dsg

    def last(v):
        return jnp.broadcast_to(v[:, T - 1 : T], (ROWS, T))

    g, dg = last(c), last(dc)
    tail = jnp.exp(g - c)
    w = tail * dt
    dw = tail * ((dg - dc) * dt + ddt)
    for k, v in (
        (K_C, c), (K_DC, dc), (K_DT, dt), (K_DDT, ddt), (K_W, w), (K_DW, dw), (K_TAIL, tail), (K_SG, sg),
        (K_DSG, dsg), (K_F0, f0), (K_F1, f1), (K_G, g), (K_DG, dg), (K_F0T, last(f0)), (K_F1T, last(f1)),
        (K_D, d_skip), (K_DD, p_skip),
    ):
        table_ref[k] = v
    total = jnp.zeros((CPD, N), F32)
    d_total = jnp.zeros((CPD, N), F32)
    for b in range(BLK):
        xt = r_ref[b, 0:CPD, :]
        bmat = r_ref[b, CPD : CPD + N, :].astype(BF16)
        parts = split(xt * heads_rows(table_ref, K_W, b)) + split(xt * heads_rows(table_ref, K_DW, b))
        got = mm(jnp.concatenate(parts, axis=0), bmat)
        s = got[0:CPD] + got[CPD : 2 * CPD]
        ds = got[2 * CPD : 3 * CPD] + got[3 * CPD :]
        s_ref[b, 0] = s
        s_ref[b, 1] = ds
        eg = jnp.exp(heads_rows(table_ref, K_G, b))
        d_total = eg * (d_total + heads_rows(table_ref, K_DG, b) * total) + ds
        total = eg * total + s
    write_message(msg_ref, total, d_total)
    write_decay(msg_ref, table_ref)


def scan_kernel(reverse, decay_ref, m_ref, o_ref):
    total = jnp.zeros((CPS, N), F32)
    d_total = jnp.zeros((CPS, N), F32)
    for i in range(SEGS - 1, -1, -1) if reverse else range(SEGS):
        o_ref[i, 0:CPS, :] = total
        o_ref[i, CPS : 2 * CPS, :] = d_total
        eg = jnp.exp(decay_ref[i, 2 * CPS : 2 * CPS + 1, :])
        dg = decay_ref[i, 2 * CPS + 1 : 2 * CPS + 2, :]
        d_total = eg * (d_total + dg * total) + m_ref[i, CPS : 2 * CPS, :]
        total = eg * total + m_ref[i, 0:CPS, :]


def scan_up_kernel(m_ref, *rest):
    scan_kernel(False, m_ref, m_ref, rest[-1])


def gains(zl_ref, *refs):
    halves = CPD // 128
    out = []
    for ref in refs:
        rows = [ref[pl.ds(zl_ref[0] * halves + i, 1), :] for i in range(halves)]
        out.append(jnp.concatenate([jnp.broadcast_to(v, (T, 128)).T for v in rows], axis=0))
    return out


def silu(z):
    return z / (1.0 + jnp.exp(-z))


def decays(table, cols, r, scores, causal):
    gap = table[K_C, r : r + 1, :] - cols[:, r : r + 1]
    d_gap = table[K_DC, r : r + 1, :] - cols[:, ROWS + r : ROWS + r + 1]
    return jnp.where(causal, scores * jnp.exp(jnp.where(causal, gap, 0.0)), 0.0), d_gap


def columns(table):
    rows = [table[k] for k in (K_C, K_DC, K_DT, K_DDT)]
    return jnp.concatenate(rows + [jnp.zeros((T - 4 * ROWS, T), F32)], axis=0).T


def causal_mask():
    return lax.broadcasted_iota(jnp.int32, (T, T), 0) <= lax.broadcasted_iota(jnp.int32, (T, T), 1)


def out_kernel(
    zl_ref, gain_in, dgain_in, r_ref, g0, g1, g2, g3, h_ref, table_ref, s_ref,
    g_ref, y_ref, hb_ref, msg_ref, sems,
):
    copies = []
    for d, src in enumerate((g0, g1, g2, g3)):
        b = lax.rem(zl_ref[0] + BLK - d, BLK)
        copies.append(pltpu.make_async_copy(src, g_ref.at[b], sems.at[d]))
        copies[-1].start()
    for copy in copies:
        copy.wait()
    causal = causal_mask()
    cols = columns(table_ref)
    gain, dgain = gains(zl_ref, gain_in, dgain_in)
    h = h_ref[:, 0:CPS, :].reshape(CPD, N)
    dh = h_ref[:, CPS : 2 * CPS, :].reshape(CPD, N)
    for b in range(BLK):
        xt = r_ref[b, 0:CPD, :]
        xb = xt.astype(BF16)
        bmat = r_ref[b, CPD : CPD + N, :].astype(BF16)
        cmat = g_ref[b, 2 * CPD : 2 * CPD + T, :].astype(BF16)
        hb_ref[b, 0] = h
        hb_ref[b, 1] = dh
        got = mmt(jnp.concatenate(split(h) + split(dh), axis=0), cmat)
        ch = got[0:CPD] + got[CPD : 2 * CPD]
        dch = got[2 * CPD : 3 * CPD] + got[3 * CPD :]
        scores = mmt(bmat, cmat)
        y_parts, dy_parts = [], []
        for i in range(HPD):
            r = b * HPD + i
            mat, d_gap = decays(table_ref, cols, r, scores, causal)
            dt = cols[:, 2 * ROWS + r : 2 * ROWS + r + 1]
            ddt = cols[:, 3 * ROWS + r : 3 * ROWS + r + 1]
            w = mat * dt
            dw = mat * (d_gap * dt + ddt)
            w_hi, w_lo = split(jnp.concatenate([w, dw], axis=1))
            x_i = xb[i * HD : (i + 1) * HD]
            inner = mm(x_i, w_hi) + mm(x_i, w_lo)
            ec = jnp.exp(table_ref[K_C, r : r + 1, :])
            dc = table_ref[K_DC, r : r + 1, :]
            ch_i, dch_i = ch[i * HD : (i + 1) * HD], dch[i * HD : (i + 1) * HD]
            y_parts.append(inner[:, :T] + ec * ch_i)
            dy_parts.append(inner[:, T:] + ec * (dc * ch_i + dch_i))
        y_nd = jnp.concatenate(y_parts, axis=0)
        dy_nd = jnp.concatenate(dy_parts, axis=0)
        y_ref[0, b] = y_nd
        y_ref[1, b] = dy_nd
        s = silu(g_ref[b, 0:CPD, :])
        cot = g_ref[b, CPD : 2 * CPD, :]
        u = (y_nd + heads_rows(table_ref, K_D, b) * xt) * s
        du = (dy_nd + heads_rows(table_ref, K_DD, b) * xt) * s
        q, dq = gain * cot, dgain * cot
        for n, v in enumerate((u * u, u * q, u * du, du * q + u * dq)):
            row = jnp.sum(v, axis=0, keepdims=True)
            for j in range(BLK):
                msg_ref[j, n * BLK + b : n * BLK + b + 1, :] = row
        eg = jnp.exp(heads_rows(table_ref, K_G, b))
        dh = eg * (dh + heads_rows(table_ref, K_DG, b) * h) + s_ref[b, 1]
        h = eg * h + s_ref[b, 0]


def seed_kernel(
    zl_ref, gain_in, dgain_in, r_ref, g_ref, n_ref, table_ref, y_ref, yb_ref, seed_ref, gain_ref, msg_ref
):
    gain, dgain = gains(zl_ref, gain_in, dgain_in)
    sums = n_ref[0] + n_ref[1] + n_ref[2] + n_ref[3]
    acc = jnp.zeros((CPD, T), F32)
    adj = jnp.zeros((CPD, N), F32)
    d_adj = jnp.zeros((CPD, N), F32)
    for b in range(BLK - 1, -1, -1):
        xt = r_ref[b, 0:CPD, :]
        cmat = g_ref[b, 2 * CPD : 2 * CPD + T, :].astype(BF16)
        s = silu(g_ref[b, 0:CPD, :])
        cot = g_ref[b, CPD : 2 * CPD, :]
        u = (y_ref[0, b] + heads_rows(table_ref, K_D, b) * xt) * s
        du = (y_ref[1, b] + heads_rows(table_ref, K_DD, b) * xt) * s
        square, m, p, dm = [sums[n * BLK + b : n * BLK + b + 1, :] for n in range(4)]
        mean = square * (1.0 / CH) + EPS
        inv = lax.rsqrt(mean)
        inv = inv * (1.5 - 0.5 * mean * inv * inv)
        cube = inv * inv * inv
        dinv = -cube * p * (1.0 / CH)
        k2 = cube * m * (1.0 / CH)
        k3 = (3.0 * inv * inv * dinv * m + cube * dm) * (1.0 / CH)
        q, dq = gain * cot, dgain * cot
        yb = s * (inv * q - k2 * u)
        dyb = s * (dinv * q + inv * dq - k3 * u - k2 * du)
        yb_ref[0, b] = yb
        yb_ref[1, b] = dyb
        acc = acc + cot * (du * inv + u * dinv)
        ec = jnp.exp(heads_rows(table_ref, K_C, b))
        e0 = ec * yb
        e1 = ec * (heads_rows(table_ref, K_DC, b) * yb + dyb)
        got = mm(jnp.concatenate(split(e0) + split(e1), axis=0), cmat)
        seed = got[0:CPD] + got[CPD : 2 * CPD]
        d_seed = got[2 * CPD : 3 * CPD] + got[3 * CPD :]
        seed_ref[b, 0] = seed
        seed_ref[b, 1] = d_seed
        eg = jnp.exp(heads_rows(table_ref, K_G, b))
        d_adj = eg * (d_adj + heads_rows(table_ref, K_DG, b) * adj) + d_seed
        adj = eg * adj + seed
    for i in range(CPD // 128):
        gain_ref[i : i + 1, :] = jnp.sum(acc[i * 128 : (i + 1) * 128].T, axis=0, keepdims=True)
    write_message(msg_ref, adj, d_adj)


def head_sum(v):
    return jnp.sum(v, axis=0, keepdims=True)


def input_kernel(
    zl_ref, r_ref, g_ref, l_ref, table_ref, y_ref, yb_ref, hb_ref, seed_ref, gain_ref, *rest
):
    o_refs, part_ref, o_ref, sems = rest[:BLK], rest[BLK], rest[BLK + 1], rest[BLK + 2]
    causal = causal_mask()
    cols = columns(table_ref)
    adj = l_ref[:, 0:CPS, :].reshape(CPD, N)
    d_adj = l_ref[:, CPS : 2 * CPS, :].reshape(CPD, N)
    acc_a = [jnp.zeros((1, T), F32) for _ in range(HPD)]
    acc_dt = [jnp.zeros((1, T), F32) for _ in range(HPD)]
    acc_skip = [jnp.zeros((1, T), F32) for _ in range(HPD)]
    for b in range(BLK - 1, -1, -1):
        bmat = r_ref[b, CPD : CPD + N, :].astype(BF16)
        cmat = g_ref[b, 2 * CPD : 2 * CPD + T, :].astype(BF16)
        got = mmt(jnp.concatenate(split(adj) + split(d_adj), axis=0), bmat)
        bl = got[0:CPD] + got[CPD : 2 * CPD]
        dbl = got[2 * CPD : 3 * CPD] + got[3 * CPD :]
        scores = mmt(bmat, cmat)
        out_parts = []
        for i in range(HPD):
            r = b * HPD + i
            rows = slice(i * HD, (i + 1) * HD)

            def row(k):
                return table_ref[k, r : r + 1, :]

            mat, d_gap = decays(table_ref, cols, r, scores, causal)
            l_hi, l_lo = split(mat)
            n_hi, n_lo = split(mat * d_gap)
            yb, dyb = yb_ref[0, b, rows, :], yb_ref[1, b, rows, :]
            y_hi, y_lo = split(yb)
            dy_hi, dy_lo = split(dyb)
            got = mmt(jnp.concatenate([y_hi, dy_hi, y_lo, dy_lo], axis=0), l_hi)
            low = mmt(jnp.concatenate([y_hi, dy_hi], axis=0), l_lo)
            both = got[: 2 * HD] + got[2 * HD :] + low
            gap_part = mmt(jnp.concatenate([y_hi, y_lo], axis=0), n_hi)
            gap_part = gap_part[:HD] + gap_part[HD:] + mmt(y_hi, n_lo)
            xt = r_ref[b, rows, :]
            bl_i, dbl_i = bl[rows], dbl[rows]
            tail, dt, ddt, dc, dg = row(K_TAIL), row(K_DT), row(K_DDT), row(K_DC), row(K_DG)
            k = both[:HD] + tail * bl_i
            dk = both[HD:] + gap_part + tail * ((dg - dc) * bl_i + dbl_i)
            out_parts.append(ddt * k + dt * dk + row(K_DD) * yb + row(K_D) * dyb)
            y_nd, dy_nd = y_ref[0, b, rows, :], y_ref[1, b, rows, :]
            xk, dxk = head_sum(xt * k), head_sum(xt * dk)
            e0 = head_sum(yb * y_nd) - dt * xk
            e1 = head_sum(dyb * y_nd + yb * dy_nd) - ddt * xk - dt * dxk
            xbl, dxbl = head_sum(xt * bl_i), head_sum(xt * dbl_i)
            h, dh = hb_ref[b, 0, rows, :], hb_ref[b, 1, rows, :]
            lam, d_lam = adj[rows], d_adj[rows]
            eg = jnp.exp(row(K_G))
            hl = eg * head_sum(lam * h)
            dhl = eg * head_sum(d_lam * h + lam * dh)
            g0 = hl + row(K_W) * xbl
            g1 = dg * hl + dhl + row(K_DW) * xbl + row(K_W) * dxbl
            acc_a[i] = acc_a[i] + dc * e0 + row(K_C) * e1 + dg * g0 + row(K_G) * g1
            acc_dt[i] = (
                acc_dt[i] + row(K_DSG) * xk + row(K_SG) * dxk + row(K_F1) * e0 + row(K_F0) * e1
                + row(K_F1T) * g0 + row(K_F0T) * g1
            )
            acc_skip[i] = acc_skip[i] + head_sum(xt * dyb)
        out = jnp.concatenate(out_parts, axis=0)
        for i in range(CPD // 128):
            o_ref[b, i * 128 : (i + 1) * 128, :] = out[i * 128 : (i + 1) * 128].T
        if b:
            eg = jnp.exp(heads_rows(table_ref, K_G, b))
            d_adj = eg * (d_adj + heads_rows(table_ref, K_DG, b) * adj) + seed_ref[b, 1]
            adj = eg * adj + seed_ref[b, 0]
    part = jnp.concatenate(acc_a + acc_dt + acc_skip + [gain_ref[...], jnp.zeros((2, T), F32)], axis=0)
    copies = []
    for d in range(BLK):
        copies.append(pltpu.make_async_copy(o_ref.at[lax.rem(zl_ref[0] + d, BLK)], o_refs[d], sems.at[d]))
        copies[-1].start()
    for i in range(NEAR):
        part_ref[i] = part
    for copy in copies:
        copy.wait()


def place_kernel(zl_ref, i0, i1, i2, i3, o_ref, sems):
    copies = []
    for d, src in enumerate((i0, i1, i2, i3)):
        j = lax.rem(zl_ref[0] + BLK - d, BLK)
        for i in range(CPD // 128):
            lo = pl.multiple_of(j * CPD + i * 128, 128)
            copies.append(
                pltpu.make_async_copy(
                    src.at[pl.ds(i * 128, 128), :], o_ref.at[:, pl.ds(lo, 128)], sems.at[len(copies)]
                )
            )
            copies[-1].start()
    for copy in copies:
        copy.wait()


def sum_kernel(m_ref, *rest):
    o_ref = rest[-1]
    total = m_ref[0]
    for i in range(1, NEAR):
        total = total + m_ref[i]
    for i in range(FAR):
        o_ref[i] = total


def finish_kernel(factor, m_ref, a_ref, dt_ref, skip_ref, gain_ref):
    outs = (a_ref, dt_ref, skip_ref)
    rows = [[] for _ in outs]
    for j in range(BLK):
        total = m_ref[j]
        for i in range(1, FAR // BLK):
            total = total + m_ref[i * BLK + j]
        total = total * factor
        for n in range(len(outs)):
            rows[n].append(total[n * HPD : (n + 1) * HPD, :])
        gain_ref[2 * j : 2 * j + 2, :] = total[3 * HPD : 3 * HPD + 2, :]
    for n, ref in enumerate(outs):
        ref[...] = jnp.sum(jnp.concatenate(rows[n], axis=0).T, axis=0, keepdims=True)


def call(kernel, name, outs, in_specs=None, scratch=(), out_specs=None):
    def shape(dims):
        return jax.ShapeDtypeStruct(dims, F32)

    many = isinstance(outs, list)
    spec = pl.BlockSpec(memory_space=pltpu.VMEM)

    def run(*args):
        return pl.pallas_call(
            kernel,
            name=name,
            out_shape=[shape(o) for o in outs] if many else shape(outs),
            out_specs=out_specs or ([spec] * len(outs) if many else spec),
            in_specs=in_specs or [spec] * len(args),
            scratch_shapes=list(scratch),
            compiler_params=pltpu.CompilerParams(vmem_limit_bytes=VMEM),
        )(*args)

    return run


def per_device(
    ssm_input,
    gate_input,
    b_proj,
    c_proj,
    dt_raw,
    cotangent,
    a_log,
    dt_bias,
    d_skip,
    norm_gain,
    probe_a,
    probe_dt,
    probe_skip,
    probe_gain,
):
    vm, sm, hbm = [pl.BlockSpec(memory_space=m) for m in (pltpu.VMEM, pltpu.SMEM, pltpu.HBM)]

    def in_hbm(v):
        return pltpu.with_memory_space_constraint(v, pltpu.HBM)

    def exchange(v, axes):
        return lax.all_to_all(v, axes, 0, 0)

    group, segs = "zl", ("y", "zh")

    def shift(v, d):
        return lax.ppermute(v, group, [(i, (i + d) % BLK) for i in range(BLK)])

    zl = lax.axis_index(group).reshape(1)
    params = jnp.stack([a_log, dt_bias, d_skip, probe_a, probe_dt, probe_skip])
    params = lax.dynamic_slice_in_dim(params, lax.axis_index(group) * HPD, HPD, 1)
    params = jnp.broadcast_to(params.reshape(PARAMS * HPD, 1), (PARAMS * HPD, T))
    gain = (norm_gain.reshape(8, 128), probe_gain.reshape(8, 128))
    packed = call(pack_x_kernel, "pack_x", (BLK, X_ROWS, T), [hbm] * 3,
        [pltpu.VMEM((T, CH), BF16), pltpu.VMEM((T, N), BF16), pltpu.VMEM((HEADS, T), F32)]
        + [pltpu.SemaphoreType.DMA((3,))],
    )(*[in_hbm(v) for v in (ssm_input, b_proj, dt_raw.T)])
    r = exchange(packed, group)
    parts = call(pack_g_kernel, "pack_g", [(G_ROWS, T)] * BLK, [sm] + [vm] * 3,
        [pltpu.VMEM((G_ROWS, T), F32)] * BLK + [pltpu.SemaphoreType.DMA((BLK,))], [hbm] * BLK,
    )(zl, gate_input, cotangent, c_proj)
    parts = [shift(v, d) if d else v for d, v in enumerate(parts)]
    table, s, msg = call(
        state_kernel,
        "state",
        [(TABLE, ROWS, T), (BLK, 2, CPD, N), (SEGS, M_ROWS, N)],
        [vm, vm] + [hbm] * len(FIRST),
    )(params, r, *[parts[d] for d in FIRST])
    decay = exchange(msg, segs)
    early = [parts[d] for d in EARLY]
    before = call(scan_up_kernel, "scan_up", (SEGS, 2 * CPS, N), [vm] + [hbm] * len(early))(decay, *early)
    h_in = exchange(before, segs)
    g, y, h_blocks, norms = call(
        out_kernel,
        "mix",
        [(BLK, G_ROWS, T), (2, BLK, CPD, T), (BLK, 2, CPD, N), (BLK, 4 * BLK, T)],
        [sm] + [vm] * 3 + [hbm] * BLK + [vm] * 3,
        [pltpu.SemaphoreType.DMA((BLK,))],
    )(zl, *gain, r, *[in_hbm(v) for v in parts], h_in, table, s)
    norms = exchange(norms, group)
    y_bar, seeds, d_gain, msg = call(
        seed_kernel,
        "seeds",
        [(2, BLK, CPD, T), (BLK, 2, CPD, N), (2, 128), (SEGS, 2 * CPS, N)],
        [sm] + [vm] * 7,
    )(zl, *gain, r, g, norms, table, y)
    after = call(functools.partial(scan_kernel, True), "scan_down", (SEGS, 2 * CPS, N))(
        decay, exchange(msg, segs)
    )
    adj = exchange(after, segs)
    *outs, part = call(
        input_kernel,
        "input_grad",
        [(CPD, 128)] * BLK + [(NEAR, 4 * HPD, T)],
        [sm] + [vm] * 9,
        [pltpu.VMEM((BLK, CPD, 128), F32), pltpu.SemaphoreType.DMA((BLK,))],
        [hbm] * BLK + [vm],
    )(zl, r, g, adj, table, y, y_bar, h_blocks, seeds, d_gain)
    outs = [shift(v, d) if d else v for d, v in enumerate(outs)]
    part = exchange(part, ("x", "core", "y"))
    early = [outs[d] for d in BACK]
    part = call(sum_kernel, "near_sum", (FAR, 4 * HPD, T), [vm] + [hbm] * len(early))(part, *early)
    hvp_input = call(
        place_kernel,
        "place",
        (T, CH),
        [sm] + [hbm] * BLK,
        [pltpu.SemaphoreType.DMA((CH // 128,))],
        hbm,
    )(zl, *outs)
    factor = 1.0 / math.sqrt(T * NEAR * FAR)
    hvp_a, hvp_dt, hvp_skip, hvp_gain = call(
        functools.partial(finish_kernel, factor), "finish", [(1, HEADS)] * 3 + [(8, 128)]
    )(exchange(part, ("zhi", "zh", "zl")))
    return (
        hvp_input,
        hvp_a.reshape(HEADS),
        hvp_dt.reshape(HEADS),
        hvp_skip.reshape(HEADS),
        hvp_gain.reshape(CH),
    )


def solution(mesh):
    axes = ("zhi", "x", "core", "y", "zh", "zl")
    fine = Mesh(mesh.devices.reshape(2, 4, 2, 4, 2, 4), axes)
    tokens = P(axes, None)
    return jax.shard_map(
        per_device,
        mesh=fine,
        in_specs=(tokens,) * 6 + (P(),) * 8,
        out_specs=(tokens, P(), P(), P(), P()),
        check_vma=False,
    )
```

```python
import functools
import math

import jax
import jax.numpy as jnp
from jax import lax
from jax.experimental import pallas as pl
from jax.experimental.pallas import tpu as pltpu
from jax.sharding import Mesh, PartitionSpec as P

F32, BF16 = jnp.float32, jnp.bfloat16
EPS = 1e-05
T = 128
N = 128
HD = 64
HEADS = 16
CH = 1024
BLK = 4
HPD = HEADS // BLK
CPD = HPD * HD
ROWS = BLK * HPD
SEGS = 8
CPS = CPD // SEGS
PARAMS = 6
PART = 8
NEAR = 32
FAR = 16
FIRST = (1,)
EARLY = (2,)
BACK = (2,)
X_ROWS = CPD + N + HPD + 4
G_ROWS = 2 * CPD + T
M_ROWS = 2 * CPS + 8
VMEM = 16 * 1024 * 1024

(K_C, K_DC, K_DT, K_DDT, K_W, K_DW, K_TAIL, K_SG, K_DSG, K_F0, K_F1, K_G, K_DG, K_F0T, K_F1T, K_D, K_DD) = range(17)
TABLE = 17


def split(a):
    hi = a.astype(BF16)
    return hi, (a - hi.astype(F32)).astype(BF16)


def mm(a, b):
    return lax.dot_general(a, b, (((1,), (0,)), ((), ())), preferred_element_type=F32)


def mmt(a, b):
    return lax.dot_general(a, b, (((1,), (1,)), ((), ())), preferred_element_type=F32)


def heads_rows(table, k, b):
    return jnp.concatenate(
        [jnp.broadcast_to(table[k, b * HPD + h : b * HPD + h + 1, :], (HD, T)) for h in range(HPD)], axis=0
    )


def pack_x_kernel(x_hbm, b_hbm, dt_hbm, o_ref, x_ref, b_ref, dt_ref, sems):
    pairs = ((x_hbm, x_ref), (b_hbm, b_ref), (dt_hbm, dt_ref))
    copies = [pltpu.make_async_copy(src, dst, sems.at[n]) for n, (src, dst) in enumerate(pairs)]
    for copy in copies:
        copy.start()
    for copy in copies:
        copy.wait()
    for j in range(BLK):
        for i in range(CPD // 128):
            lo = j * CPD + i * 128
            o_ref[j, i * 128 : (i + 1) * 128, :] = x_ref[:, lo : lo + 128].astype(F32).T
        o_ref[j, CPD : CPD + N, :] = b_ref[...].astype(F32)
        at = CPD + N
        o_ref[j, at : at + HPD, :] = dt_ref[j * HPD : (j + 1) * HPD, :]
        at += HPD
        o_ref[j, at:X_ROWS, :] = jnp.zeros((X_ROWS - at, T), F32)


def pack_g_kernel(zl_ref, z_ref, cot_ref, c_ref, *rest):
    o_refs, made, sems = rest[:BLK], rest[BLK : 2 * BLK], rest[2 * BLK]
    copies = [pltpu.make_async_copy(made[d], o_refs[d], sems.at[d]) for d in range(BLK)]
    for d in (*range(1, BLK), 0):
        o_ref = made[d]
        j = lax.rem(zl_ref[0] + d, BLK)
        for n, ref in enumerate((z_ref, cot_ref)):
            for i in range(CPD // 128):
                lo = pl.multiple_of(j * CPD + i * 128, 128)
                at = n * CPD + i * 128
                o_ref[at : at + 128, :] = ref[:, pl.ds(lo, 128)].astype(F32).T
        o_ref[2 * CPD : 2 * CPD + T, :] = c_ref[...].astype(F32)
        copies[d].start()
    for copy in copies:
        copy.wait()


def write_message(msg_ref, total, d_total):
    for j in range(SEGS):
        msg_ref[j, 0:CPS, :] = total[j * CPS : (j + 1) * CPS]
        msg_ref[j, CPS : 2 * CPS, :] = d_total[j * CPS : (j + 1) * CPS]


def write_decay(msg_ref, table):
    for j in range(SEGS):
        h = j * CPS // HD
        g, dg = None, None
        for b in range(BLK):
            r = b * HPD + h
            g_b, dg_b = table[K_G, r : r + 1, :], table[K_DG, r : r + 1, :]
            g, dg = (g_b, dg_b) if g is None else (g + g_b, dg + dg_b)
        msg_ref[j, 2 * CPS : 2 * CPS + 1, :] = g
        msg_ref[j, 2 * CPS + 1 : 2 * CPS + 2, :] = dg
        msg_ref[j, 2 * CPS + 2 : M_ROWS, :] = jnp.zeros((M_ROWS - 2 * CPS - 2, T), F32)


def state_kernel(prm_ref, r_ref, *rest):
    table_ref, s_ref, msg_ref = rest[-3:]
    at = CPD + N
    raw = jnp.concatenate([r_ref[b, at : at + HPD, :] for b in range(BLK)], axis=0)

    a_log, dt_bias, d_skip, p_a, p_dt, p_skip = [
        jnp.concatenate([prm_ref[k * HPD : (k + 1) * HPD, :]] * BLK, axis=0) for k in range(PARAMS)
    ]
    pre = raw + dt_bias
    dt = jnp.maximum(pre, 0.0) + jnp.log1p(jnp.exp(-jnp.abs(pre)))
    sg = 1.0 / (1.0 + jnp.exp(-pre))
    dsg = sg * (1.0 - sg) * p_dt
    ddt = sg * p_dt
    a = -jnp.exp(a_log)
    da = a * p_a
    before = lax.broadcasted_iota(jnp.int32, (T, T), 0) <= lax.broadcasted_iota(jnp.int32, (T, T), 1)
    sums = lax.dot_general(
        jnp.concatenate([dt, sg, dsg], axis=0),
        jnp.where(before, 1.0, 0.0).astype(F32),
        (((1,), (0,)), ((), ())),
        precision=lax.Precision.HIGHEST,
        preferred_element_type=F32,
    )
    cum_dt, cum_sg, cum_dsg = sums[:ROWS], sums[ROWS : 2 * ROWS], sums[2 * ROWS :]
    c = a * cum_dt
    dc = da * cum_dt + a * p_dt * cum_sg
    f0 = a * cum_sg
    f1 = da * cum_sg + a * cum_dsg

    def last(v):
        return jnp.broadcast_to(v[:, T - 1 : T], (ROWS, T))

    g, dg = last(c), last(dc)
    tail = jnp.exp(g - c)
    w = tail * dt
    dw = tail * ((dg - dc) * dt + ddt)
    for k, v in (
        (K_C, c), (K_DC, dc), (K_DT, dt), (K_DDT, ddt), (K_W, w), (K_DW, dw), (K_TAIL, tail), (K_SG, sg),
        (K_DSG, dsg), (K_F0, f0), (K_F1, f1), (K_G, g), (K_DG, dg), (K_F0T, last(f0)), (K_F1T, last(f1)),
        (K_D, d_skip), (K_DD, p_skip),
    ):
        table_ref[k] = v
    total = jnp.zeros((CPD, N), F32)
    d_total = jnp.zeros((CPD, N), F32)
    for b in range(BLK):
        xt = r_ref[b, 0:CPD, :]
        bmat = r_ref[b, CPD : CPD + N, :].astype(BF16)
        parts = split(xt * heads_rows(table_ref, K_W, b)) + split(xt * heads_rows(table_ref, K_DW, b))
        got = mm(jnp.concatenate(parts, axis=0), bmat)
        s = got[0:CPD] + got[CPD : 2 * CPD]
        ds = got[2 * CPD : 3 * CPD] + got[3 * CPD :]
        s_ref[b, 0] = s
        s_ref[b, 1] = ds
        eg = jnp.exp(heads_rows(table_ref, K_G, b))
        d_total = eg * (d_total + heads_rows(table_ref, K_DG, b) * total) + ds
        total = eg * total + s
    write_message(msg_ref, total, d_total)
    write_decay(msg_ref, table_ref)


def scan_kernel(reverse, decay_ref, m_ref, o_ref):
    total = jnp.zeros((CPS, N), F32)
    d_total = jnp.zeros((CPS, N), F32)
    for n in range(SEGS - 1, -1, -1) if reverse else range(SEGS):
        i = n % 2 * (SEGS // 2) + n // 2
        o_ref[i, 0:CPS, :] = total
        o_ref[i, CPS : 2 * CPS, :] = d_total
        eg = jnp.exp(decay_ref[i, 2 * CPS : 2 * CPS + 1, :])
        dg = decay_ref[i, 2 * CPS + 1 : 2 * CPS + 2, :]
        d_total = eg * (d_total + dg * total) + m_ref[i, CPS : 2 * CPS, :]
        total = eg * total + m_ref[i, 0:CPS, :]


def scan_up_kernel(m_ref, *rest):
    scan_kernel(False, m_ref, m_ref, rest[-1])


def gains(zl_ref, *refs):
    halves = CPD // 128
    out = []
    for ref in refs:
        rows = [ref[pl.ds(zl_ref[0] * halves + i, 1), :] for i in range(halves)]
        out.append(jnp.concatenate([jnp.broadcast_to(v, (T, 128)).T for v in rows], axis=0))
    return out


def silu(z):
    return z / (1.0 + jnp.exp(-z))


def decays(table, cols, r, scores, causal):
    gap = table[K_C, r : r + 1, :] - cols[:, r : r + 1]
    d_gap = table[K_DC, r : r + 1, :] - cols[:, ROWS + r : ROWS + r + 1]
    return jnp.where(causal, scores * jnp.exp(jnp.where(causal, gap, 0.0)), 0.0), d_gap


def columns(table):
    rows = [table[k] for k in (K_C, K_DC, K_DT, K_DDT)]
    return jnp.concatenate(rows + [jnp.zeros((T - 4 * ROWS, T), F32)], axis=0).T


def causal_mask():
    return lax.broadcasted_iota(jnp.int32, (T, T), 0) <= lax.broadcasted_iota(jnp.int32, (T, T), 1)


def out_kernel(
    zl_ref, gain_in, dgain_in, r_ref, g0, g1, g2, g3, h_ref, table_ref, s_ref,
    g_ref, y_ref, hb_ref, msg_ref, sems,
):
    copies = []
    for d, src in enumerate((g0, g1, g2, g3)):
        b = lax.rem(zl_ref[0] + BLK - d, BLK)
        copies.append(pltpu.make_async_copy(src, g_ref.at[b], sems.at[d]))
        copies[-1].start()
    for copy in copies:
        copy.wait()
    causal = causal_mask()
    cols = columns(table_ref)
    gain, dgain = gains(zl_ref, gain_in, dgain_in)
    h = h_ref[:, 0:CPS, :].reshape(CPD, N)
    dh = h_ref[:, CPS : 2 * CPS, :].reshape(CPD, N)
    for b in range(BLK):
        xt = r_ref[b, 0:CPD, :]
        xb = xt.astype(BF16)
        bmat = r_ref[b, CPD : CPD + N, :].astype(BF16)
        cmat = g_ref[b, 2 * CPD : 2 * CPD + T, :].astype(BF16)
        hb_ref[b, 0] = h
        hb_ref[b, 1] = dh
        got = mmt(jnp.concatenate(split(h) + split(dh), axis=0), cmat)
        ch = got[0:CPD] + got[CPD : 2 * CPD]
        dch = got[2 * CPD : 3 * CPD] + got[3 * CPD :]
        scores = mmt(bmat, cmat)
        y_parts, dy_parts = [], []
        for i in range(HPD):
            r = b * HPD + i
            mat, d_gap = decays(table_ref, cols, r, scores, causal)
            dt = cols[:, 2 * ROWS + r : 2 * ROWS + r + 1]
            ddt = cols[:, 3 * ROWS + r : 3 * ROWS + r + 1]
            w = mat * dt
            dw = mat * (d_gap * dt + ddt)
            w_hi, w_lo = split(jnp.concatenate([w, dw], axis=1))
            x_i = xb[i * HD : (i + 1) * HD]
            inner = mm(x_i, w_hi) + mm(x_i, w_lo)
            ec = jnp.exp(table_ref[K_C, r : r + 1, :])
            dc = table_ref[K_DC, r : r + 1, :]
            ch_i, dch_i = ch[i * HD : (i + 1) * HD], dch[i * HD : (i + 1) * HD]
            y_parts.append(inner[:, :T] + ec * ch_i)
            dy_parts.append(inner[:, T:] + ec * (dc * ch_i + dch_i))
        y_nd = jnp.concatenate(y_parts, axis=0)
        dy_nd = jnp.concatenate(dy_parts, axis=0)
        y_ref[0, b] = y_nd
        y_ref[1, b] = dy_nd
        s = silu(g_ref[b, 0:CPD, :])
        cot = g_ref[b, CPD : 2 * CPD, :]
        u = (y_nd + heads_rows(table_ref, K_D, b) * xt) * s
        du = (dy_nd + heads_rows(table_ref, K_DD, b) * xt) * s
        q, dq = gain * cot, dgain * cot
        for n, v in enumerate((u * u, u * q, u * du, du * q + u * dq)):
            row = jnp.sum(v, axis=0, keepdims=True)
            for j in range(BLK):
                msg_ref[j, n * BLK + b : n * BLK + b + 1, :] = row
        eg = jnp.exp(heads_rows(table_ref, K_G, b))
        dh = eg * (dh + heads_rows(table_ref, K_DG, b) * h) + s_ref[b, 1]
        h = eg * h + s_ref[b, 0]


def seed_kernel(
    zl_ref, gain_in, dgain_in, r_ref, g_ref, n_ref, table_ref, y_ref, yb_ref, seed_ref, gain_ref, msg_ref
):
    gain, dgain = gains(zl_ref, gain_in, dgain_in)
    sums = n_ref[0] + n_ref[1] + n_ref[2] + n_ref[3]
    acc = jnp.zeros((CPD, T), F32)
    adj = jnp.zeros((CPD, N), F32)
    d_adj = jnp.zeros((CPD, N), F32)
    for b in range(BLK - 1, -1, -1):
        xt = r_ref[b, 0:CPD, :]
        cmat = g_ref[b, 2 * CPD : 2 * CPD + T, :].astype(BF16)
        s = silu(g_ref[b, 0:CPD, :])
        cot = g_ref[b, CPD : 2 * CPD, :]
        u = (y_ref[0, b] + heads_rows(table_ref, K_D, b) * xt) * s
        du = (y_ref[1, b] + heads_rows(table_ref, K_DD, b) * xt) * s
        square, m, p, dm = [sums[n * BLK + b : n * BLK + b + 1, :] for n in range(4)]
        mean = square * (1.0 / CH) + EPS
        inv = lax.rsqrt(mean)
        inv = inv * (1.5 - 0.5 * mean * inv * inv)
        cube = inv * inv * inv
        dinv = -cube * p * (1.0 / CH)
        k2 = cube * m * (1.0 / CH)
        k3 = (3.0 * inv * inv * dinv * m + cube * dm) * (1.0 / CH)
        q, dq = gain * cot, dgain * cot
        yb = s * (inv * q - k2 * u)
        dyb = s * (dinv * q + inv * dq - k3 * u - k2 * du)
        yb_ref[0, b] = yb
        yb_ref[1, b] = dyb
        acc = acc + cot * (du * inv + u * dinv)
        ec = jnp.exp(heads_rows(table_ref, K_C, b))
        e0 = ec * yb
        e1 = ec * (heads_rows(table_ref, K_DC, b) * yb + dyb)
        got = mm(jnp.concatenate(split(e0) + split(e1), axis=0), cmat)
        seed = got[0:CPD] + got[CPD : 2 * CPD]
        d_seed = got[2 * CPD : 3 * CPD] + got[3 * CPD :]
        seed_ref[b, 0] = seed
        seed_ref[b, 1] = d_seed
        eg = jnp.exp(heads_rows(table_ref, K_G, b))
        d_adj = eg * (d_adj + heads_rows(table_ref, K_DG, b) * adj) + d_seed
        adj = eg * adj + seed
    for i in range(CPD // 128):
        gain_ref[i : i + 1, :] = jnp.sum(acc[i * 128 : (i + 1) * 128].T, axis=0, keepdims=True)
    write_message(msg_ref, adj, d_adj)


def head_sum(v):
    return jnp.sum(v, axis=0, keepdims=True)


def input_kernel(
    zl_ref, r_ref, g_ref, l_ref, table_ref, y_ref, yb_ref, hb_ref, seed_ref, gain_ref, *rest
):
    o_refs, part_ref, o_ref, sems = rest[:BLK], rest[BLK], rest[BLK + 1], rest[BLK + 2]
    causal = causal_mask()
    cols = columns(table_ref)
    adj = l_ref[:, 0:CPS, :].reshape(CPD, N)
    d_adj = l_ref[:, CPS : 2 * CPS, :].reshape(CPD, N)
    acc_a = [jnp.zeros((1, T), F32) for _ in range(HPD)]
    acc_dt = [jnp.zeros((1, T), F32) for _ in range(HPD)]
    acc_skip = [jnp.zeros((1, T), F32) for _ in range(HPD)]
    for b in range(BLK - 1, -1, -1):
        bmat = r_ref[b, CPD : CPD + N, :].astype(BF16)
        cmat = g_ref[b, 2 * CPD : 2 * CPD + T, :].astype(BF16)
        got = mmt(jnp.concatenate(split(adj) + split(d_adj), axis=0), bmat)
        bl = got[0:CPD] + got[CPD : 2 * CPD]
        dbl = got[2 * CPD : 3 * CPD] + got[3 * CPD :]
        scores = mmt(bmat, cmat)
        out_parts = []
        for i in range(HPD):
            r = b * HPD + i
            rows = slice(i * HD, (i + 1) * HD)

            def row(k):
                return table_ref[k, r : r + 1, :]

            mat, d_gap = decays(table_ref, cols, r, scores, causal)
            l_hi, l_lo = split(mat)
            n_hi, n_lo = split(mat * d_gap)
            yb, dyb = yb_ref[0, b, rows, :], yb_ref[1, b, rows, :]
            y_hi, y_lo = split(yb)
            dy_hi, dy_lo = split(dyb)
            got = mmt(jnp.concatenate([y_hi, dy_hi, y_lo, dy_lo], axis=0), l_hi)
            low = mmt(jnp.concatenate([y_hi, dy_hi], axis=0), l_lo)
            both = got[: 2 * HD] + got[2 * HD :] + low
            gap_part = mmt(jnp.concatenate([y_hi, y_lo], axis=0), n_hi)
            gap_part = gap_part[:HD] + gap_part[HD:] + mmt(y_hi, n_lo)
            xt = r_ref[b, rows, :]
            bl_i, dbl_i = bl[rows], dbl[rows]
            tail, dt, ddt, dc, dg = row(K_TAIL), row(K_DT), row(K_DDT), row(K_DC), row(K_DG)
            k = both[:HD] + tail * bl_i
            dk = both[HD:] + gap_part + tail * ((dg - dc) * bl_i + dbl_i)
            out_parts.append(ddt * k + dt * dk + row(K_DD) * yb + row(K_D) * dyb)
            y_nd, dy_nd = y_ref[0, b, rows, :], y_ref[1, b, rows, :]
            xk, dxk = head_sum(xt * k), head_sum(xt * dk)
            e0 = head_sum(yb * y_nd) - dt * xk
            e1 = head_sum(dyb * y_nd + yb * dy_nd) - ddt * xk - dt * dxk
            xbl, dxbl = head_sum(xt * bl_i), head_sum(xt * dbl_i)
            h, dh = hb_ref[b, 0, rows, :], hb_ref[b, 1, rows, :]
            lam, d_lam = adj[rows], d_adj[rows]
            eg = jnp.exp(row(K_G))
            hl = eg * head_sum(lam * h)
            dhl = eg * head_sum(d_lam * h + lam * dh)
            g0 = hl + row(K_W) * xbl
            g1 = dg * hl + dhl + row(K_DW) * xbl + row(K_W) * dxbl
            acc_a[i] = acc_a[i] + dc * e0 + row(K_C) * e1 + dg * g0 + row(K_G) * g1
            acc_dt[i] = (
                acc_dt[i] + row(K_DSG) * xk + row(K_SG) * dxk + row(K_F1) * e0 + row(K_F0) * e1
                + row(K_F1T) * g0 + row(K_F0T) * g1
            )
            acc_skip[i] = acc_skip[i] + head_sum(xt * dyb)
        out = jnp.concatenate(out_parts, axis=0)
        for i in range(CPD // 128):
            o_ref[b, i * 128 : (i + 1) * 128, :] = out[i * 128 : (i + 1) * 128].T
        if b:
            eg = jnp.exp(heads_rows(table_ref, K_G, b))
            d_adj = eg * (d_adj + heads_rows(table_ref, K_DG, b) * adj) + seed_ref[b, 1]
            adj = eg * adj + seed_ref[b, 0]
    sums = jnp.concatenate(acc_a + acc_dt + acc_skip + [jnp.zeros((T - 3 * HPD, T), F32)], axis=0)
    sums = jnp.sum(sums.T, axis=0, keepdims=True)
    part = jnp.concatenate([gain_ref[...], sums, jnp.zeros((PART - 3, T), F32)], axis=0)
    copies = []
    for d in range(BLK):
        copies.append(pltpu.make_async_copy(o_ref.at[lax.rem(zl_ref[0] + d, BLK)], o_refs[d], sems.at[d]))
        copies[-1].start()
    for i in range(NEAR):
        part_ref[i] = part
    for copy in copies:
        copy.wait()


def place_kernel(zl_ref, i0, i1, i2, i3, o_ref, sems):
    copies = []
    for d, src in enumerate((i0, i1, i2, i3)):
        j = lax.rem(zl_ref[0] + BLK - d, BLK)
        for i in range(CPD // 128):
            lo = pl.multiple_of(j * CPD + i * 128, 128)
            copies.append(
                pltpu.make_async_copy(
                    src.at[pl.ds(i * 128, 128), :], o_ref.at[:, pl.ds(lo, 128)], sems.at[len(copies)]
                )
            )
            copies[-1].start()
    for copy in copies:
        copy.wait()


def sum_kernel(m_ref, *rest):
    o_ref = rest[-1]
    total = m_ref[0]
    for i in range(1, NEAR):
        total = total + m_ref[i]
    for i in range(FAR):
        o_ref[i] = total


def finish_kernel(factor, m_ref, gain_ref, *head_refs):
    heads = []
    for j in range(BLK):
        total = m_ref[j]
        for i in range(1, FAR // BLK):
            total = total + m_ref[i * BLK + j]
        total = total * factor
        gain_ref[2 * j : 2 * j + 2, :] = total[0:2, :]
        heads.append(total[2:3, :])
    for n, ref in enumerate(head_refs):
        ref[...] = jnp.concatenate([v[:, n * HPD : (n + 1) * HPD] for v in heads], axis=1)


def call(kernel, name, outs, in_specs=None, scratch=(), out_specs=None):
    def shape(dims):
        return jax.ShapeDtypeStruct(dims, F32)

    many = isinstance(outs, list)
    spec = pl.BlockSpec(memory_space=pltpu.VMEM)

    def run(*args):
        return pl.pallas_call(
            kernel,
            name=name,
            out_shape=[shape(o) for o in outs] if many else shape(outs),
            out_specs=out_specs or ([spec] * len(outs) if many else spec),
            in_specs=in_specs or [spec] * len(args),
            scratch_shapes=list(scratch),
            compiler_params=pltpu.CompilerParams(vmem_limit_bytes=VMEM),
        )(*args)

    return run


def per_device(
    ssm_input,
    gate_input,
    b_proj,
    c_proj,
    dt_raw,
    cotangent,
    a_log,
    dt_bias,
    d_skip,
    norm_gain,
    probe_a,
    probe_dt,
    probe_skip,
    probe_gain,
):
    vm, sm, hbm = [pl.BlockSpec(memory_space=m) for m in (pltpu.VMEM, pltpu.SMEM, pltpu.HBM)]

    def in_hbm(v):
        return pltpu.with_memory_space_constraint(v, pltpu.HBM)

    def exchange(v, axes):
        return lax.all_to_all(v, axes, 0, 0)

    group, segs = "zl", ("zh", "y")

    def shift(v, d):
        return lax.ppermute(v, group, [(i, (i + d) % BLK) for i in range(BLK)])

    zl = lax.axis_index(group).reshape(1)
    params = jnp.stack([a_log, dt_bias, d_skip, probe_a, probe_dt, probe_skip])
    params = lax.dynamic_slice_in_dim(params, lax.axis_index(group) * HPD, HPD, 1)
    params = jnp.broadcast_to(params.reshape(PARAMS * HPD, 1), (PARAMS * HPD, T))
    gain = (norm_gain.reshape(8, 128), probe_gain.reshape(8, 128))
    packed = call(pack_x_kernel, "pack_x", (BLK, X_ROWS, T), [hbm] * 3,
        [pltpu.VMEM((T, CH), BF16), pltpu.VMEM((T, N), BF16), pltpu.VMEM((HEADS, T), F32)]
        + [pltpu.SemaphoreType.DMA((3,))],
    )(*[in_hbm(v) for v in (ssm_input, b_proj, dt_raw.T)])
    r = exchange(packed, group)
    parts = call(pack_g_kernel, "pack_g", [(G_ROWS, T)] * BLK, [sm] + [vm] * 3,
        [pltpu.VMEM((G_ROWS, T), F32)] * BLK + [pltpu.SemaphoreType.DMA((BLK,))], [hbm] * BLK,
    )(zl, gate_input, cotangent, c_proj)
    parts = [shift(v, d) if d else v for d, v in enumerate(parts)]
    table, s, msg = call(
        state_kernel,
        "state",
        [(TABLE, ROWS, T), (BLK, 2, CPD, N), (SEGS, M_ROWS, N)],
        [vm, vm] + [hbm] * len(FIRST),
    )(params, r, *[parts[d] for d in FIRST])
    decay = exchange(msg, segs)
    early = [parts[d] for d in EARLY]
    before = call(scan_up_kernel, "scan_up", (SEGS, 2 * CPS, N), [vm] + [hbm] * len(early))(decay, *early)
    h_in = exchange(before, segs)
    g, y, h_blocks, norms = call(
        out_kernel,
        "mix",
        [(BLK, G_ROWS, T), (2, BLK, CPD, T), (BLK, 2, CPD, N), (BLK, 4 * BLK, T)],
        [sm] + [vm] * 3 + [hbm] * BLK + [vm] * 3,
        [pltpu.SemaphoreType.DMA((BLK,))],
    )(zl, *gain, r, *[in_hbm(v) for v in parts], h_in, table, s)
    norms = exchange(norms, group)
    y_bar, seeds, d_gain, msg = call(
        seed_kernel,
        "seeds",
        [(2, BLK, CPD, T), (BLK, 2, CPD, N), (2, 128), (SEGS, 2 * CPS, N)],
        [sm] + [vm] * 7,
    )(zl, *gain, r, g, norms, table, y)
    after = call(functools.partial(scan_kernel, True), "scan_down", (SEGS, 2 * CPS, N))(
        decay, exchange(msg, segs)
    )
    adj = exchange(after, segs)
    *outs, part = call(
        input_kernel,
        "input_grad",
        [(CPD, 128)] * BLK + [(NEAR, PART, T)],
        [sm] + [vm] * 9,
        [pltpu.VMEM((BLK, CPD, 128), F32), pltpu.SemaphoreType.DMA((BLK,))],
        [hbm] * BLK + [vm],
    )(zl, r, g, adj, table, y, y_bar, h_blocks, seeds, d_gain)
    outs = [shift(v, d) if d else v for d, v in enumerate(outs)]
    part = exchange(part, ("x", "core", "y"))
    early = [outs[d] for d in BACK]
    part = call(sum_kernel, "near_sum", (FAR, PART, T), [vm] + [hbm] * len(early))(part, *early)
    hvp_input = call(
        place_kernel,
        "place",
        (T, CH),
        [sm] + [hbm] * BLK,
        [pltpu.SemaphoreType.DMA((CH // 128,))],
        hbm,
    )(zl, *outs)
    factor = 1.0 / math.sqrt(T * NEAR * FAR)
    hvp_gain, *heads = call(functools.partial(finish_kernel, factor), "finish", [(8, 128)] + [(1, HEADS)] * 3)(
        exchange(part, ("zhi", "zh", "zl"))
    )
    return (
        hvp_input,
        *[v.reshape(HEADS) for v in heads],
        hvp_gain.reshape(CH),
    )


def solution(mesh):
    axes = ("zhi", "x", "core", "y", "zh", "zl")
    fine = Mesh(mesh.devices.reshape(2, 4, 2, 4, 2, 4), axes)
    tokens = P(axes, None)
    return jax.shard_map(
        per_device,
        mesh=fine,
        in_specs=(tokens,) * 6 + (P(),) * 8,
        out_specs=(tokens, P(), P(), P(), P()),
        check_vma=False,
    )
```

```python
import functools
import math

import jax
import jax.numpy as jnp
from jax import lax
from jax.experimental import pallas as pl
from jax.experimental.pallas import tpu as pltpu
from jax.sharding import Mesh, PartitionSpec as P

F32, BF16 = jnp.float32, jnp.bfloat16
EPS = 1e-05
T = 128
N = 128
HD = 64
HEADS = 16
CH = 1024
BLK = 4
HPD = HEADS // BLK
CPD = HPD * HD
ROWS = BLK * HPD
SEGS = 8
CPS = CPD // SEGS
PARAMS = 6
PART = 8
NEAR = 32
FAR = 16
FIRST = (1,)
EARLY = (2,)
BACK = (2,)
X_ROWS = CPD + N + T + HPD + 4
G_ROWS = 2 * CPD
M_ROWS = 2 * CPS + 8
VMEM = 16 * 1024 * 1024

(K_C, K_DC, K_DT, K_DDT, K_W, K_DW, K_TAIL, K_SG, K_DSG, K_F0, K_F1, K_G, K_DG, K_F0T, K_F1T, K_D, K_DD) = range(17)
TABLE = 17


def split(a):
    hi = a.astype(BF16)
    return hi, (a - hi.astype(F32)).astype(BF16)


def mm(a, b):
    return lax.dot_general(a, b, (((1,), (0,)), ((), ())), preferred_element_type=F32)


def mmt(a, b):
    return lax.dot_general(a, b, (((1,), (1,)), ((), ())), preferred_element_type=F32)


def heads_rows(table, k, b):
    return jnp.concatenate(
        [jnp.broadcast_to(table[k, b * HPD + h : b * HPD + h + 1, :], (HD, T)) for h in range(HPD)], axis=0
    )


def pack_x_kernel(x_hbm, b_hbm, dt_hbm, c_hbm, o_ref, x_ref, b_ref, dt_ref, c_ref, sems):
    pairs = ((x_hbm, x_ref), (b_hbm, b_ref), (dt_hbm, dt_ref), (c_hbm, c_ref))
    copies = [pltpu.make_async_copy(src, dst, sems.at[n]) for n, (src, dst) in enumerate(pairs)]
    for copy in copies:
        copy.start()
    for copy in copies:
        copy.wait()
    for j in range(BLK):
        for i in range(CPD // 128):
            lo = j * CPD + i * 128
            o_ref[j, i * 128 : (i + 1) * 128, :] = x_ref[:, lo : lo + 128].astype(F32).T
        o_ref[j, CPD : CPD + N, :] = b_ref[...].astype(F32)
        o_ref[j, CPD + N : CPD + N + T, :] = c_ref[...].astype(F32)
        at = CPD + N + T
        o_ref[j, at : at + HPD, :] = dt_ref[j * HPD : (j + 1) * HPD, :]
        at += HPD
        o_ref[j, at:X_ROWS, :] = jnp.zeros((X_ROWS - at, T), F32)


def pack_g_kernel(zl_ref, z_ref, cot_ref, *rest):
    o_refs, made, sems = rest[:BLK], rest[BLK : 2 * BLK], rest[2 * BLK]
    copies = [pltpu.make_async_copy(made[d], o_refs[d], sems.at[d]) for d in range(BLK)]
    for d in (*range(1, BLK), 0):
        o_ref = made[d]
        j = lax.rem(zl_ref[0] + d, BLK)
        for n, ref in enumerate((z_ref, cot_ref)):
            for i in range(CPD // 128):
                lo = pl.multiple_of(j * CPD + i * 128, 128)
                at = n * CPD + i * 128
                o_ref[at : at + 128, :] = ref[:, pl.ds(lo, 128)].astype(F32).T
        copies[d].start()
    for copy in copies:
        copy.wait()


def write_message(msg_ref, total, d_total):
    for j in range(SEGS):
        msg_ref[j, 0:CPS, :] = total[j * CPS : (j + 1) * CPS]
        msg_ref[j, CPS : 2 * CPS, :] = d_total[j * CPS : (j + 1) * CPS]


def write_decay(msg_ref, table):
    for j in range(SEGS):
        h = j * CPS // HD
        g, dg = None, None
        for b in range(BLK):
            r = b * HPD + h
            g_b, dg_b = table[K_G, r : r + 1, :], table[K_DG, r : r + 1, :]
            g, dg = (g_b, dg_b) if g is None else (g + g_b, dg + dg_b)
        msg_ref[j, 2 * CPS : 2 * CPS + 1, :] = g
        msg_ref[j, 2 * CPS + 1 : 2 * CPS + 2, :] = dg
        msg_ref[j, 2 * CPS + 2 : M_ROWS, :] = jnp.zeros((M_ROWS - 2 * CPS - 2, T), F32)


def state_kernel(prm_ref, r_ref, *rest):
    table_ref, s_ref, msg_ref = rest[-3:]
    at = CPD + N + T
    raw = jnp.concatenate([r_ref[b, at : at + HPD, :] for b in range(BLK)], axis=0)

    a_log, dt_bias, d_skip, p_a, p_dt, p_skip = [
        jnp.concatenate([prm_ref[k * HPD : (k + 1) * HPD, :]] * BLK, axis=0) for k in range(PARAMS)
    ]
    pre = raw + dt_bias
    dt = jnp.maximum(pre, 0.0) + jnp.log1p(jnp.exp(-jnp.abs(pre)))
    sg = 1.0 / (1.0 + jnp.exp(-pre))
    dsg = sg * (1.0 - sg) * p_dt
    ddt = sg * p_dt
    a = -jnp.exp(a_log)
    da = a * p_a
    before = lax.broadcasted_iota(jnp.int32, (T, T), 0) <= lax.broadcasted_iota(jnp.int32, (T, T), 1)
    sums = lax.dot_general(
        jnp.concatenate([dt, sg, dsg], axis=0),
        jnp.where(before, 1.0, 0.0).astype(F32),
        (((1,), (0,)), ((), ())),
        precision=lax.Precision.HIGHEST,
        preferred_element_type=F32,
    )
    cum_dt, cum_sg, cum_dsg = sums[:ROWS], sums[ROWS : 2 * ROWS], sums[2 * ROWS :]
    c = a * cum_dt
    dc = da * cum_dt + a * p_dt * cum_sg
    f0 = a * cum_sg
    f1 = da * cum_sg + a * cum_dsg

    def last(v):
        return jnp.broadcast_to(v[:, T - 1 : T], (ROWS, T))

    g, dg = last(c), last(dc)
    tail = jnp.exp(g - c)
    w = tail * dt
    dw = tail * ((dg - dc) * dt + ddt)
    for k, v in (
        (K_C, c), (K_DC, dc), (K_DT, dt), (K_DDT, ddt), (K_W, w), (K_DW, dw), (K_TAIL, tail), (K_SG, sg),
        (K_DSG, dsg), (K_F0, f0), (K_F1, f1), (K_G, g), (K_DG, dg), (K_F0T, last(f0)), (K_F1T, last(f1)),
        (K_D, d_skip), (K_DD, p_skip),
    ):
        table_ref[k] = v
    total = jnp.zeros((CPD, N), F32)
    d_total = jnp.zeros((CPD, N), F32)
    for b in range(BLK):
        xt = r_ref[b, 0:CPD, :]
        bmat = r_ref[b, CPD : CPD + N, :].astype(BF16)
        parts = split(xt * heads_rows(table_ref, K_W, b)) + split(xt * heads_rows(table_ref, K_DW, b))
        got = mm(jnp.concatenate(parts, axis=0), bmat)
        s = got[0:CPD] + got[CPD : 2 * CPD]
        ds = got[2 * CPD : 3 * CPD] + got[3 * CPD :]
        s_ref[b, 0] = s
        s_ref[b, 1] = ds
        eg = jnp.exp(heads_rows(table_ref, K_G, b))
        d_total = eg * (d_total + heads_rows(table_ref, K_DG, b) * total) + ds
        total = eg * total + s
    write_message(msg_ref, total, d_total)
    write_decay(msg_ref, table_ref)


def scan_kernel(reverse, decay_ref, m_ref, o_ref):
    total = jnp.zeros((CPS, N), F32)
    d_total = jnp.zeros((CPS, N), F32)
    for n in range(SEGS - 1, -1, -1) if reverse else range(SEGS):
        i = n % 2 * (SEGS // 2) + n // 2
        o_ref[i, 0:CPS, :] = total
        o_ref[i, CPS : 2 * CPS, :] = d_total
        eg = jnp.exp(decay_ref[i, 2 * CPS : 2 * CPS + 1, :])
        dg = decay_ref[i, 2 * CPS + 1 : 2 * CPS + 2, :]
        d_total = eg * (d_total + dg * total) + m_ref[i, CPS : 2 * CPS, :]
        total = eg * total + m_ref[i, 0:CPS, :]


def scan_up_kernel(m_ref, *rest):
    scan_kernel(False, m_ref, m_ref, rest[-1])


def gains(zl_ref, *refs):
    halves = CPD // 128
    out = []
    for ref in refs:
        rows = [ref[pl.ds(zl_ref[0] * halves + i, 1), :] for i in range(halves)]
        out.append(jnp.concatenate([jnp.broadcast_to(v, (T, 128)).T for v in rows], axis=0))
    return out


def silu(z):
    return z / (1.0 + jnp.exp(-z))


def decays(table, cols, r, scores, causal):
    gap = table[K_C, r : r + 1, :] - cols[:, r : r + 1]
    d_gap = table[K_DC, r : r + 1, :] - cols[:, ROWS + r : ROWS + r + 1]
    return jnp.where(causal, scores * jnp.exp(jnp.where(causal, gap, 0.0)), 0.0), d_gap


def columns(table):
    rows = [table[k] for k in (K_C, K_DC, K_DT, K_DDT)]
    return jnp.concatenate(rows + [jnp.zeros((T - 4 * ROWS, T), F32)], axis=0).T


def causal_mask():
    return lax.broadcasted_iota(jnp.int32, (T, T), 0) <= lax.broadcasted_iota(jnp.int32, (T, T), 1)


def out_kernel(
    zl_ref, gain_in, dgain_in, r_ref, g0, g1, g2, g3, h_ref, table_ref, s_ref,
    g_ref, y_ref, hb_ref, msg_ref, sems,
):
    copies = []
    for d, src in enumerate((g0, g1, g2, g3)):
        b = lax.rem(zl_ref[0] + BLK - d, BLK)
        copies.append(pltpu.make_async_copy(src, g_ref.at[b], sems.at[d]))
        copies[-1].start()
    for copy in copies:
        copy.wait()
    causal = causal_mask()
    cols = columns(table_ref)
    gain, dgain = gains(zl_ref, gain_in, dgain_in)
    h = h_ref[:, 0:CPS, :].reshape(CPD, N)
    dh = h_ref[:, CPS : 2 * CPS, :].reshape(CPD, N)
    for b in range(BLK):
        xt = r_ref[b, 0:CPD, :]
        xb = xt.astype(BF16)
        bmat = r_ref[b, CPD : CPD + N, :].astype(BF16)
        cmat = r_ref[b, CPD + N : CPD + N + T, :].astype(BF16)
        hb_ref[b, 0] = h
        hb_ref[b, 1] = dh
        got = mmt(jnp.concatenate(split(h) + split(dh), axis=0), cmat)
        ch = got[0:CPD] + got[CPD : 2 * CPD]
        dch = got[2 * CPD : 3 * CPD] + got[3 * CPD :]
        scores = mmt(bmat, cmat)
        y_parts, dy_parts = [], []
        for i in range(HPD):
            r = b * HPD + i
            mat, d_gap = decays(table_ref, cols, r, scores, causal)
            dt = cols[:, 2 * ROWS + r : 2 * ROWS + r + 1]
            ddt = cols[:, 3 * ROWS + r : 3 * ROWS + r + 1]
            w = mat * dt
            dw = mat * (d_gap * dt + ddt)
            w_hi, w_lo = split(jnp.concatenate([w, dw], axis=1))
            x_i = xb[i * HD : (i + 1) * HD]
            inner = mm(x_i, w_hi) + mm(x_i, w_lo)
            ec = jnp.exp(table_ref[K_C, r : r + 1, :])
            dc = table_ref[K_DC, r : r + 1, :]
            ch_i, dch_i = ch[i * HD : (i + 1) * HD], dch[i * HD : (i + 1) * HD]
            y_parts.append(inner[:, :T] + ec * ch_i)
            dy_parts.append(inner[:, T:] + ec * (dc * ch_i + dch_i))
        y_nd = jnp.concatenate(y_parts, axis=0)
        dy_nd = jnp.concatenate(dy_parts, axis=0)
        y_ref[0, b] = y_nd
        y_ref[1, b] = dy_nd
        s = silu(g_ref[b, 0:CPD, :])
        cot = g_ref[b, CPD : 2 * CPD, :]
        u = (y_nd + heads_rows(table_ref, K_D, b) * xt) * s
        du = (dy_nd + heads_rows(table_ref, K_DD, b) * xt) * s
        q, dq = gain * cot, dgain * cot
        for n, v in enumerate((u * u, u * q, u * du, du * q + u * dq)):
            row = jnp.sum(v, axis=0, keepdims=True)
            for j in range(BLK):
                msg_ref[j, n * BLK + b : n * BLK + b + 1, :] = row
        eg = jnp.exp(heads_rows(table_ref, K_G, b))
        dh = eg * (dh + heads_rows(table_ref, K_DG, b) * h) + s_ref[b, 1]
        h = eg * h + s_ref[b, 0]


def seed_kernel(
    zl_ref, gain_in, dgain_in, r_ref, g_ref, n_ref, table_ref, y_ref, yb_ref, seed_ref, gain_ref, msg_ref
):
    gain, dgain = gains(zl_ref, gain_in, dgain_in)
    sums = n_ref[0] + n_ref[1] + n_ref[2] + n_ref[3]
    acc = jnp.zeros((CPD, T), F32)
    adj = jnp.zeros((CPD, N), F32)
    d_adj = jnp.zeros((CPD, N), F32)
    for b in range(BLK - 1, -1, -1):
        xt = r_ref[b, 0:CPD, :]
        cmat = r_ref[b, CPD + N : CPD + N + T, :].astype(BF16)
        s = silu(g_ref[b, 0:CPD, :])
        cot = g_ref[b, CPD : 2 * CPD, :]
        u = (y_ref[0, b] + heads_rows(table_ref, K_D, b) * xt) * s
        du = (y_ref[1, b] + heads_rows(table_ref, K_DD, b) * xt) * s
        square, m, p, dm = [sums[n * BLK + b : n * BLK + b + 1, :] for n in range(4)]
        mean = square * (1.0 / CH) + EPS
        inv = lax.rsqrt(mean)
        inv = inv * (1.5 - 0.5 * mean * inv * inv)
        cube = inv * inv * inv
        dinv = -cube * p * (1.0 / CH)
        k2 = cube * m * (1.0 / CH)
        k3 = (3.0 * inv * inv * dinv * m + cube * dm) * (1.0 / CH)
        q, dq = gain * cot, dgain * cot
        yb = s * (inv * q - k2 * u)
        dyb = s * (dinv * q + inv * dq - k3 * u - k2 * du)
        yb_ref[0, b] = yb
        yb_ref[1, b] = dyb
        acc = acc + cot * (du * inv + u * dinv)
        ec = jnp.exp(heads_rows(table_ref, K_C, b))
        e0 = ec * yb
        e1 = ec * (heads_rows(table_ref, K_DC, b) * yb + dyb)
        got = mm(jnp.concatenate(split(e0) + split(e1), axis=0), cmat)
        seed = got[0:CPD] + got[CPD : 2 * CPD]
        d_seed = got[2 * CPD : 3 * CPD] + got[3 * CPD :]
        seed_ref[b, 0] = seed
        seed_ref[b, 1] = d_seed
        eg = jnp.exp(heads_rows(table_ref, K_G, b))
        d_adj = eg * (d_adj + heads_rows(table_ref, K_DG, b) * adj) + d_seed
        adj = eg * adj + seed
    for i in range(CPD // 128):
        gain_ref[i : i + 1, :] = jnp.sum(acc[i * 128 : (i + 1) * 128].T, axis=0, keepdims=True)
    write_message(msg_ref, adj, d_adj)


def head_sum(v):
    return jnp.sum(v, axis=0, keepdims=True)


def input_kernel(
    zl_ref, r_ref, g_ref, l_ref, table_ref, y_ref, yb_ref, hb_ref, seed_ref, gain_ref, *rest
):
    o_refs, part_ref, o_ref, sems = rest[:BLK], rest[BLK], rest[BLK + 1], rest[BLK + 2]
    causal = causal_mask()
    cols = columns(table_ref)
    adj = l_ref[:, 0:CPS, :].reshape(CPD, N)
    d_adj = l_ref[:, CPS : 2 * CPS, :].reshape(CPD, N)
    acc_a = [jnp.zeros((1, T), F32) for _ in range(HPD)]
    acc_dt = [jnp.zeros((1, T), F32) for _ in range(HPD)]
    acc_skip = [jnp.zeros((1, T), F32) for _ in range(HPD)]
    for b in range(BLK - 1, -1, -1):
        bmat = r_ref[b, CPD : CPD + N, :].astype(BF16)
        cmat = r_ref[b, CPD + N : CPD + N + T, :].astype(BF16)
        got = mmt(jnp.concatenate(split(adj) + split(d_adj), axis=0), bmat)
        bl = got[0:CPD] + got[CPD : 2 * CPD]
        dbl = got[2 * CPD : 3 * CPD] + got[3 * CPD :]
        scores = mmt(bmat, cmat)
        out_parts = []
        for i in range(HPD):
            r = b * HPD + i
            rows = slice(i * HD, (i + 1) * HD)

            def row(k):
                return table_ref[k, r : r + 1, :]

            mat, d_gap = decays(table_ref, cols, r, scores, causal)
            l_hi, l_lo = split(mat)
            n_hi, n_lo = split(mat * d_gap)
            yb, dyb = yb_ref[0, b, rows, :], yb_ref[1, b, rows, :]
            y_hi, y_lo = split(yb)
            dy_hi, dy_lo = split(dyb)
            got = mmt(jnp.concatenate([y_hi, dy_hi, y_lo, dy_lo], axis=0), l_hi)
            low = mmt(jnp.concatenate([y_hi, dy_hi], axis=0), l_lo)
            both = got[: 2 * HD] + got[2 * HD :] + low
            gap_part = mmt(jnp.concatenate([y_hi, y_lo], axis=0), n_hi)
            gap_part = gap_part[:HD] + gap_part[HD:] + mmt(y_hi, n_lo)
            xt = r_ref[b, rows, :]
            bl_i, dbl_i = bl[rows], dbl[rows]
            tail, dt, ddt, dc, dg = row(K_TAIL), row(K_DT), row(K_DDT), row(K_DC), row(K_DG)
            k = both[:HD] + tail * bl_i
            dk = both[HD:] + gap_part + tail * ((dg - dc) * bl_i + dbl_i)
            out_parts.append(ddt * k + dt * dk + row(K_DD) * yb + row(K_D) * dyb)
            y_nd, dy_nd = y_ref[0, b, rows, :], y_ref[1, b, rows, :]
            xk, dxk = head_sum(xt * k), head_sum(xt * dk)
            e0 = head_sum(yb * y_nd) - dt * xk
            e1 = head_sum(dyb * y_nd + yb * dy_nd) - ddt * xk - dt * dxk
            xbl, dxbl = head_sum(xt * bl_i), head_sum(xt * dbl_i)
            h, dh = hb_ref[b, 0, rows, :], hb_ref[b, 1, rows, :]
            lam, d_lam = adj[rows], d_adj[rows]
            eg = jnp.exp(row(K_G))
            hl = eg * head_sum(lam * h)
            dhl = eg * head_sum(d_lam * h + lam * dh)
            g0 = hl + row(K_W) * xbl
            g1 = dg * hl + dhl + row(K_DW) * xbl + row(K_W) * dxbl
            acc_a[i] = acc_a[i] + dc * e0 + row(K_C) * e1 + dg * g0 + row(K_G) * g1
            acc_dt[i] = (
                acc_dt[i] + row(K_DSG) * xk + row(K_SG) * dxk + row(K_F1) * e0 + row(K_F0) * e1
                + row(K_F1T) * g0 + row(K_F0T) * g1
            )
            acc_skip[i] = acc_skip[i] + head_sum(xt * dyb)
        out = jnp.concatenate(out_parts, axis=0)
        for i in range(CPD // 128):
            o_ref[b, i * 128 : (i + 1) * 128, :] = out[i * 128 : (i + 1) * 128].T
        if b:
            eg = jnp.exp(heads_rows(table_ref, K_G, b))
            d_adj = eg * (d_adj + heads_rows(table_ref, K_DG, b) * adj) + seed_ref[b, 1]
            adj = eg * adj + seed_ref[b, 0]
    sums = jnp.concatenate(acc_a + acc_dt + acc_skip + [jnp.zeros((T - 3 * HPD, T), F32)], axis=0)
    sums = jnp.sum(sums.T, axis=0, keepdims=True)
    part = jnp.concatenate([gain_ref[...], sums, jnp.zeros((PART - 3, T), F32)], axis=0)
    copies = []
    for d in range(BLK):
        copies.append(pltpu.make_async_copy(o_ref.at[lax.rem(zl_ref[0] + d, BLK)], o_refs[d], sems.at[d]))
        copies[-1].start()
    for i in range(NEAR):
        part_ref[i] = part
    for copy in copies:
        copy.wait()


def place_kernel(zl_ref, i0, i1, i2, i3, o_ref, sems):
    copies = []
    for d, src in enumerate((i0, i1, i2, i3)):
        j = lax.rem(zl_ref[0] + BLK - d, BLK)
        for i in range(CPD // 128):
            lo = pl.multiple_of(j * CPD + i * 128, 128)
            copies.append(
                pltpu.make_async_copy(
                    src.at[pl.ds(i * 128, 128), :], o_ref.at[:, pl.ds(lo, 128)], sems.at[len(copies)]
                )
            )
            copies[-1].start()
    for copy in copies:
        copy.wait()


def sum_kernel(m_ref, *rest):
    o_ref = rest[-1]
    total = m_ref[0]
    for i in range(1, NEAR):
        total = total + m_ref[i]
    for i in range(FAR):
        o_ref[i] = total


def finish_kernel(factor, m_ref, gain_ref, *head_refs):
    heads = []
    for j in range(BLK):
        total = m_ref[j]
        for i in range(1, FAR // BLK):
            total = total + m_ref[i * BLK + j]
        total = total * factor
        gain_ref[2 * j : 2 * j + 2, :] = total[0:2, :]
        heads.append(total[2:3, :])
    for n, ref in enumerate(head_refs):
        ref[...] = jnp.concatenate([v[:, n * HPD : (n + 1) * HPD] for v in heads], axis=1)


def call(kernel, name, outs, in_specs=None, scratch=(), out_specs=None):
    def shape(dims):
        return jax.ShapeDtypeStruct(dims, F32)

    many = isinstance(outs, list)
    spec = pl.BlockSpec(memory_space=pltpu.VMEM)

    def run(*args):
        return pl.pallas_call(
            kernel,
            name=name,
            out_shape=[shape(o) for o in outs] if many else shape(outs),
            out_specs=out_specs or ([spec] * len(outs) if many else spec),
            in_specs=in_specs or [spec] * len(args),
            scratch_shapes=list(scratch),
            compiler_params=pltpu.CompilerParams(vmem_limit_bytes=VMEM),
        )(*args)

    return run


def per_device(
    ssm_input,
    gate_input,
    b_proj,
    c_proj,
    dt_raw,
    cotangent,
    a_log,
    dt_bias,
    d_skip,
    norm_gain,
    probe_a,
    probe_dt,
    probe_skip,
    probe_gain,
):
    vm, sm, hbm = [pl.BlockSpec(memory_space=m) for m in (pltpu.VMEM, pltpu.SMEM, pltpu.HBM)]

    def in_hbm(v):
        return pltpu.with_memory_space_constraint(v, pltpu.HBM)

    def exchange(v, axes):
        return lax.all_to_all(v, axes, 0, 0)

    group, segs = "zl", ("zh", "y")

    def shift(v, d):
        return lax.ppermute(v, group, [(i, (i + d) % BLK) for i in range(BLK)])

    zl = lax.axis_index(group).reshape(1)
    params = jnp.stack([a_log, dt_bias, d_skip, probe_a, probe_dt, probe_skip])
    params = lax.dynamic_slice_in_dim(params, lax.axis_index(group) * HPD, HPD, 1)
    params = jnp.broadcast_to(params.reshape(PARAMS * HPD, 1), (PARAMS * HPD, T))
    gain = (norm_gain.reshape(8, 128), probe_gain.reshape(8, 128))
    packed = call(pack_x_kernel, "pack_x", (BLK, X_ROWS, T), [hbm] * 4,
        [pltpu.VMEM((T, CH), BF16), pltpu.VMEM((T, N), BF16), pltpu.VMEM((HEADS, T), F32), pltpu.VMEM((T, N), BF16)]
        + [pltpu.SemaphoreType.DMA((4,))],
    )(*[in_hbm(v) for v in (ssm_input, b_proj, dt_raw.T, c_proj)])
    r = exchange(packed, group)
    parts = call(pack_g_kernel, "pack_g", [(G_ROWS, T)] * BLK, [sm] + [vm] * 2,
        [pltpu.VMEM((G_ROWS, T), F32)] * BLK + [pltpu.SemaphoreType.DMA((BLK,))], [hbm] * BLK,
    )(zl, gate_input, cotangent)
    parts = [shift(v, d) if d else v for d, v in enumerate(parts)]
    table, s, msg = call(
        state_kernel,
        "state",
        [(TABLE, ROWS, T), (BLK, 2, CPD, N), (SEGS, M_ROWS, N)],
        [vm, vm] + [hbm] * len(FIRST),
    )(params, r, *[parts[d] for d in FIRST])
    decay = exchange(msg, segs)
    early = [parts[d] for d in EARLY]
    before = call(scan_up_kernel, "scan_up", (SEGS, 2 * CPS, N), [vm] + [hbm] * len(early))(decay, *early)
    h_in = exchange(before, segs)
    g, y, h_blocks, norms = call(
        out_kernel,
        "mix",
        [(BLK, G_ROWS, T), (2, BLK, CPD, T), (BLK, 2, CPD, N), (BLK, 4 * BLK, T)],
        [sm] + [vm] * 3 + [hbm] * BLK + [vm] * 3,
        [pltpu.SemaphoreType.DMA((BLK,))],
    )(zl, *gain, r, *[in_hbm(v) for v in parts], h_in, table, s)
    norms = exchange(norms, group)
    y_bar, seeds, d_gain, msg = call(
        seed_kernel,
        "seeds",
        [(2, BLK, CPD, T), (BLK, 2, CPD, N), (2, 128), (SEGS, 2 * CPS, N)],
        [sm] + [vm] * 7,
    )(zl, *gain, r, g, norms, table, y)
    after = call(functools.partial(scan_kernel, True), "scan_down", (SEGS, 2 * CPS, N))(
        decay, exchange(msg, segs)
    )
    adj = exchange(after, segs)
    *outs, part = call(
        input_kernel,
        "input_grad",
        [(CPD, 128)] * BLK + [(NEAR, PART, T)],
        [sm] + [vm] * 9,
        [pltpu.VMEM((BLK, CPD, 128), F32), pltpu.SemaphoreType.DMA((BLK,))],
        [hbm] * BLK + [vm],
    )(zl, r, g, adj, table, y, y_bar, h_blocks, seeds, d_gain)
    outs = [shift(v, d) if d else v for d, v in enumerate(outs)]
    part = exchange(part, ("x", "core", "y"))
    early = [outs[d] for d in BACK]
    part = call(sum_kernel, "near_sum", (FAR, PART, T), [vm] + [hbm] * len(early))(part, *early)
    hvp_input = call(
        place_kernel,
        "place",
        (T, CH),
        [sm] + [hbm] * BLK,
        [pltpu.SemaphoreType.DMA((CH // 128,))],
        hbm,
    )(zl, *outs)
    factor = 1.0 / math.sqrt(T * NEAR * FAR)
    hvp_gain, *heads = call(functools.partial(finish_kernel, factor), "finish", [(8, 128)] + [(1, HEADS)] * 3)(
        exchange(part, ("zhi", "zh", "zl"))
    )
    return (
        hvp_input,
        *[v.reshape(HEADS) for v in heads],
        hvp_gain.reshape(CH),
    )


def solution(mesh):
    axes = ("zhi", "x", "core", "y", "zh", "zl")
    fine = Mesh(mesh.devices.reshape(2, 4, 2, 4, 2, 4), axes)
    tokens = P(axes, None)
    return jax.shard_map(
        per_device,
        mesh=fine,
        in_specs=(tokens,) * 6 + (P(),) * 8,
        out_specs=(tokens, P(), P(), P(), P()),
        check_vma=False,
    )
```

```python
import functools
import math

import jax
import jax.numpy as jnp
from jax import lax
from jax.experimental import pallas as pl
from jax.experimental.pallas import tpu as pltpu
from jax.sharding import Mesh, PartitionSpec as P

F32, BF16 = jnp.float32, jnp.bfloat16
EPS = 1e-05
T = 128
N = 128
HD = 64
HEADS = 16
CH = 1024
BLK = 4
HPD = HEADS // BLK
CPD = HPD * HD
ROWS = BLK * HPD
SEGS = 8
CPS = CPD // SEGS
PARAMS = 6
PART = 8
NEAR = 32
FAR = 16
FIRST = (1,)
EARLY = (2, 3)
BACK = (2,)
X_ROWS = CPD + N + T + HPD + 4
G_ROWS = 2 * CPD
M_ROWS = 2 * CPS + 8
VMEM = 16 * 1024 * 1024

(K_C, K_DC, K_DT, K_DDT, K_W, K_DW, K_TAIL, K_SG, K_DSG, K_F0, K_F1, K_G, K_DG, K_F0T, K_F1T, K_D, K_DD) = range(17)
TABLE = 17


def split(a):
    hi = a.astype(BF16)
    return hi, (a - hi.astype(F32)).astype(BF16)


def mm(a, b):
    return lax.dot_general(a, b, (((1,), (0,)), ((), ())), preferred_element_type=F32)


def mmt(a, b):
    return lax.dot_general(a, b, (((1,), (1,)), ((), ())), preferred_element_type=F32)


def heads_rows(table, k, b):
    return jnp.concatenate(
        [jnp.broadcast_to(table[k, b * HPD + h : b * HPD + h + 1, :], (HD, T)) for h in range(HPD)], axis=0
    )


def pack_x_kernel(x_hbm, b_hbm, dt_hbm, c_hbm, o_ref, x_ref, b_ref, dt_ref, c_ref, sems):
    pairs = ((x_hbm, x_ref), (b_hbm, b_ref), (dt_hbm, dt_ref), (c_hbm, c_ref))
    copies = [pltpu.make_async_copy(src, dst, sems.at[n]) for n, (src, dst) in enumerate(pairs)]
    for copy in copies:
        copy.start()
    for copy in copies:
        copy.wait()
    for j in range(BLK):
        for i in range(CPD // 128):
            lo = j * CPD + i * 128
            o_ref[j, i * 128 : (i + 1) * 128, :] = x_ref[:, lo : lo + 128].astype(F32).T
        o_ref[j, CPD : CPD + N, :] = b_ref[...].astype(F32)
        o_ref[j, CPD + N : CPD + N + T, :] = c_ref[...].astype(F32)
        at = CPD + N + T
        o_ref[j, at : at + HPD, :] = dt_ref[j * HPD : (j + 1) * HPD, :]
        at += HPD
        o_ref[j, at:X_ROWS, :] = jnp.zeros((X_ROWS - at, T), F32)


def pack_g_kernel(zl_ref, z_ref, cot_ref, *rest):
    o_refs, made, sems = rest[:BLK], rest[BLK : 2 * BLK], rest[2 * BLK]
    copies = [pltpu.make_async_copy(made[d], o_refs[d], sems.at[d]) for d in range(BLK)]
    for d in (*range(1, BLK), 0):
        o_ref = made[d]
        j = lax.rem(zl_ref[0] + d, BLK)
        for n, ref in enumerate((z_ref, cot_ref)):
            for i in range(CPD // 128):
                lo = pl.multiple_of(j * CPD + i * 128, 128)
                at = n * CPD + i * 128
                o_ref[at : at + 128, :] = ref[:, pl.ds(lo, 128)].astype(F32).T
        copies[d].start()
    for copy in copies:
        copy.wait()


def write_message(msg_ref, total, d_total):
    for j in range(SEGS):
        msg_ref[j, 0:CPS, :] = total[j * CPS : (j + 1) * CPS]
        msg_ref[j, CPS : 2 * CPS, :] = d_total[j * CPS : (j + 1) * CPS]


def write_decay(msg_ref, table):
    for j in range(SEGS):
        h = j * CPS // HD
        g, dg = None, None
        for b in range(BLK):
            r = b * HPD + h
            g_b, dg_b = table[K_G, r : r + 1, :], table[K_DG, r : r + 1, :]
            g, dg = (g_b, dg_b) if g is None else (g + g_b, dg + dg_b)
        msg_ref[j, 2 * CPS : 2 * CPS + 1, :] = g
        msg_ref[j, 2 * CPS + 1 : 2 * CPS + 2, :] = dg
        msg_ref[j, 2 * CPS + 2 : M_ROWS, :] = jnp.zeros((M_ROWS - 2 * CPS - 2, T), F32)


def state_kernel(prm_ref, r_ref, *rest):
    table_ref, s_ref, msg_ref = rest[-3:]
    at = CPD + N + T
    raw = jnp.concatenate([r_ref[b, at : at + HPD, :] for b in range(BLK)], axis=0)

    a_log, dt_bias, d_skip, p_a, p_dt, p_skip = [
        jnp.concatenate([prm_ref[k * HPD : (k + 1) * HPD, :]] * BLK, axis=0) for k in range(PARAMS)
    ]
    pre = raw + dt_bias
    dt = jnp.maximum(pre, 0.0) + jnp.log1p(jnp.exp(-jnp.abs(pre)))
    sg = 1.0 / (1.0 + jnp.exp(-pre))
    dsg = sg * (1.0 - sg) * p_dt
    ddt = sg * p_dt
    a = -jnp.exp(a_log)
    da = a * p_a
    before = lax.broadcasted_iota(jnp.int32, (T, T), 0) <= lax.broadcasted_iota(jnp.int32, (T, T), 1)
    sums = lax.dot_general(
        jnp.concatenate([dt, sg, dsg], axis=0),
        jnp.where(before, 1.0, 0.0).astype(F32),
        (((1,), (0,)), ((), ())),
        precision=lax.Precision.HIGHEST,
        preferred_element_type=F32,
    )
    cum_dt, cum_sg, cum_dsg = sums[:ROWS], sums[ROWS : 2 * ROWS], sums[2 * ROWS :]
    c = a * cum_dt
    dc = da * cum_dt + a * p_dt * cum_sg
    f0 = a * cum_sg
    f1 = da * cum_sg + a * cum_dsg

    def last(v):
        return jnp.broadcast_to(v[:, T - 1 : T], (ROWS, T))

    g, dg = last(c), last(dc)
    tail = jnp.exp(g - c)
    w = tail * dt
    dw = tail * ((dg - dc) * dt + ddt)
    for k, v in (
        (K_C, c), (K_DC, dc), (K_DT, dt), (K_DDT, ddt), (K_W, w), (K_DW, dw), (K_TAIL, tail), (K_SG, sg),
        (K_DSG, dsg), (K_F0, f0), (K_F1, f1), (K_G, g), (K_DG, dg), (K_F0T, last(f0)), (K_F1T, last(f1)),
        (K_D, d_skip), (K_DD, p_skip),
    ):
        table_ref[k] = v
    total = jnp.zeros((CPD, N), F32)
    d_total = jnp.zeros((CPD, N), F32)
    for b in range(BLK):
        xt = r_ref[b, 0:CPD, :]
        bmat = r_ref[b, CPD : CPD + N, :].astype(BF16)
        parts = split(xt * heads_rows(table_ref, K_W, b)) + split(xt * heads_rows(table_ref, K_DW, b))
        got = mm(jnp.concatenate(parts, axis=0), bmat)
        s = got[0:CPD] + got[CPD : 2 * CPD]
        ds = got[2 * CPD : 3 * CPD] + got[3 * CPD :]
        s_ref[b, 0] = s
        s_ref[b, 1] = ds
        eg = jnp.exp(heads_rows(table_ref, K_G, b))
        d_total = eg * (d_total + heads_rows(table_ref, K_DG, b) * total) + ds
        total = eg * total + s
    write_message(msg_ref, total, d_total)
    write_decay(msg_ref, table_ref)


def scan_kernel(reverse, decay_ref, m_ref, o_ref):
    total = jnp.zeros((CPS, N), F32)
    d_total = jnp.zeros((CPS, N), F32)
    for n in range(SEGS - 1, -1, -1) if reverse else range(SEGS):
        i = n % 2 * (SEGS // 2) + n // 2
        o_ref[i, 0:CPS, :] = total
        o_ref[i, CPS : 2 * CPS, :] = d_total
        eg = jnp.exp(decay_ref[i, 2 * CPS : 2 * CPS + 1, :])
        dg = decay_ref[i, 2 * CPS + 1 : 2 * CPS + 2, :]
        d_total = eg * (d_total + dg * total) + m_ref[i, CPS : 2 * CPS, :]
        total = eg * total + m_ref[i, 0:CPS, :]


def scan_up_kernel(m_ref, *rest):
    scan_kernel(False, m_ref, m_ref, rest[-1])


def gains(zl_ref, *refs):
    halves = CPD // 128
    out = []
    for ref in refs:
        rows = [ref[pl.ds(zl_ref[0] * halves + i, 1), :] for i in range(halves)]
        out.append(jnp.concatenate([jnp.broadcast_to(v, (T, 128)).T for v in rows], axis=0))
    return out


def silu(z):
    return z / (1.0 + jnp.exp(-z))


def decays(table, cols, r, scores, causal):
    gap = table[K_C, r : r + 1, :] - cols[:, r : r + 1]
    d_gap = table[K_DC, r : r + 1, :] - cols[:, ROWS + r : ROWS + r + 1]
    return jnp.where(causal, scores * jnp.exp(jnp.where(causal, gap, 0.0)), 0.0), d_gap


def columns(table):
    rows = [table[k] for k in (K_C, K_DC, K_DT, K_DDT)]
    return jnp.concatenate(rows + [jnp.zeros((T - 4 * ROWS, T), F32)], axis=0).T


def causal_mask():
    return lax.broadcasted_iota(jnp.int32, (T, T), 0) <= lax.broadcasted_iota(jnp.int32, (T, T), 1)


def out_kernel(
    zl_ref, gain_in, dgain_in, r_ref, g0, g1, g2, g3, h_ref, table_ref, s_ref,
    g_ref, y_ref, hb_ref, msg_ref, sems,
):
    copies = []
    for d, src in enumerate((g0, g1, g2, g3)):
        b = lax.rem(zl_ref[0] + BLK - d, BLK)
        copies.append(pltpu.make_async_copy(src, g_ref.at[b], sems.at[d]))
        copies[-1].start()
    for copy in copies:
        copy.wait()
    causal = causal_mask()
    cols = columns(table_ref)
    gain, dgain = gains(zl_ref, gain_in, dgain_in)
    h = h_ref[:, 0:CPS, :].reshape(CPD, N)
    dh = h_ref[:, CPS : 2 * CPS, :].reshape(CPD, N)
    for b in range(BLK):
        xt = r_ref[b, 0:CPD, :]
        xb = xt.astype(BF16)
        bmat = r_ref[b, CPD : CPD + N, :].astype(BF16)
        cmat = r_ref[b, CPD + N : CPD + N + T, :].astype(BF16)
        hb_ref[b, 0] = h
        hb_ref[b, 1] = dh
        got = mmt(jnp.concatenate(split(h) + split(dh), axis=0), cmat)
        ch = got[0:CPD] + got[CPD : 2 * CPD]
        dch = got[2 * CPD : 3 * CPD] + got[3 * CPD :]
        scores = mmt(bmat, cmat)
        y_parts, dy_parts = [], []
        for i in range(HPD):
            r = b * HPD + i
            mat, d_gap = decays(table_ref, cols, r, scores, causal)
            dt = cols[:, 2 * ROWS + r : 2 * ROWS + r + 1]
            ddt = cols[:, 3 * ROWS + r : 3 * ROWS + r + 1]
            w = mat * dt
            dw = mat * (d_gap * dt + ddt)
            w_hi, w_lo = split(jnp.concatenate([w, dw], axis=1))
            x_i = xb[i * HD : (i + 1) * HD]
            inner = mm(x_i, w_hi) + mm(x_i, w_lo)
            ec = jnp.exp(table_ref[K_C, r : r + 1, :])
            dc = table_ref[K_DC, r : r + 1, :]
            ch_i, dch_i = ch[i * HD : (i + 1) * HD], dch[i * HD : (i + 1) * HD]
            y_parts.append(inner[:, :T] + ec * ch_i)
            dy_parts.append(inner[:, T:] + ec * (dc * ch_i + dch_i))
        y_nd = jnp.concatenate(y_parts, axis=0)
        dy_nd = jnp.concatenate(dy_parts, axis=0)
        y_ref[0, b] = y_nd
        y_ref[1, b] = dy_nd
        s = silu(g_ref[b, 0:CPD, :])
        cot = g_ref[b, CPD : 2 * CPD, :]
        u = (y_nd + heads_rows(table_ref, K_D, b) * xt) * s
        du = (dy_nd + heads_rows(table_ref, K_DD, b) * xt) * s
        q, dq = gain * cot, dgain * cot
        for n, v in enumerate((u * u, u * q, u * du, du * q + u * dq)):
            row = jnp.sum(v, axis=0, keepdims=True)
            for j in range(BLK):
                msg_ref[j, n * BLK + b : n * BLK + b + 1, :] = row
        eg = jnp.exp(heads_rows(table_ref, K_G, b))
        dh = eg * (dh + heads_rows(table_ref, K_DG, b) * h) + s_ref[b, 1]
        h = eg * h + s_ref[b, 0]


def seed_kernel(
    zl_ref, gain_in, dgain_in, r_ref, g_ref, n_ref, table_ref, y_ref, yb_ref, seed_ref, gain_ref, msg_ref
):
    gain, dgain = gains(zl_ref, gain_in, dgain_in)
    sums = n_ref[0] + n_ref[1] + n_ref[2] + n_ref[3]
    acc = jnp.zeros((CPD, T), F32)
    adj = jnp.zeros((CPD, N), F32)
    d_adj = jnp.zeros((CPD, N), F32)
    for b in range(BLK - 1, -1, -1):
        xt = r_ref[b, 0:CPD, :]
        cmat = r_ref[b, CPD + N : CPD + N + T, :].astype(BF16)
        s = silu(g_ref[b, 0:CPD, :])
        cot = g_ref[b, CPD : 2 * CPD, :]
        u = (y_ref[0, b] + heads_rows(table_ref, K_D, b) * xt) * s
        du = (y_ref[1, b] + heads_rows(table_ref, K_DD, b) * xt) * s
        square, m, p, dm = [sums[n * BLK + b : n * BLK + b + 1, :] for n in range(4)]
        mean = square * (1.0 / CH) + EPS
        inv = lax.rsqrt(mean)
        inv = inv * (1.5 - 0.5 * mean * inv * inv)
        cube = inv * inv * inv
        dinv = -cube * p * (1.0 / CH)
        k2 = cube * m * (1.0 / CH)
        k3 = (3.0 * inv * inv * dinv * m + cube * dm) * (1.0 / CH)
        q, dq = gain * cot, dgain * cot
        yb = s * (inv * q - k2 * u)
        dyb = s * (dinv * q + inv * dq - k3 * u - k2 * du)
        yb_ref[0, b] = yb
        yb_ref[1, b] = dyb
        acc = acc + cot * (du * inv + u * dinv)
        ec = jnp.exp(heads_rows(table_ref, K_C, b))
        e0 = ec * yb
        e1 = ec * (heads_rows(table_ref, K_DC, b) * yb + dyb)
        got = mm(jnp.concatenate(split(e0) + split(e1), axis=0), cmat)
        seed = got[0:CPD] + got[CPD : 2 * CPD]
        d_seed = got[2 * CPD : 3 * CPD] + got[3 * CPD :]
        seed_ref[b, 0] = seed
        seed_ref[b, 1] = d_seed
        eg = jnp.exp(heads_rows(table_ref, K_G, b))
        d_adj = eg * (d_adj + heads_rows(table_ref, K_DG, b) * adj) + d_seed
        adj = eg * adj + seed
    for i in range(CPD // 128):
        gain_ref[i : i + 1, :] = jnp.sum(acc[i * 128 : (i + 1) * 128].T, axis=0, keepdims=True)
    write_message(msg_ref, adj, d_adj)


def head_sum(v):
    return jnp.sum(v, axis=0, keepdims=True)


def input_kernel(
    zl_ref, r_ref, g_ref, l_ref, table_ref, y_ref, yb_ref, hb_ref, seed_ref, gain_ref, *rest
):
    o_refs, part_ref, o_ref, sems = rest[:BLK], rest[BLK], rest[BLK + 1], rest[BLK + 2]
    causal = causal_mask()
    cols = columns(table_ref)
    adj = l_ref[:, 0:CPS, :].reshape(CPD, N)
    d_adj = l_ref[:, CPS : 2 * CPS, :].reshape(CPD, N)
    acc_a = [jnp.zeros((1, T), F32) for _ in range(HPD)]
    acc_dt = [jnp.zeros((1, T), F32) for _ in range(HPD)]
    acc_skip = [jnp.zeros((1, T), F32) for _ in range(HPD)]
    for b in range(BLK - 1, -1, -1):
        bmat = r_ref[b, CPD : CPD + N, :].astype(BF16)
        cmat = r_ref[b, CPD + N : CPD + N + T, :].astype(BF16)
        got = mmt(jnp.concatenate(split(adj) + split(d_adj), axis=0), bmat)
        bl = got[0:CPD] + got[CPD : 2 * CPD]
        dbl = got[2 * CPD : 3 * CPD] + got[3 * CPD :]
        scores = mmt(bmat, cmat)
        out_parts = []
        for i in range(HPD):
            r = b * HPD + i
            rows = slice(i * HD, (i + 1) * HD)

            def row(k):
                return table_ref[k, r : r + 1, :]

            mat, d_gap = decays(table_ref, cols, r, scores, causal)
            l_hi, l_lo = split(mat)
            n_hi, n_lo = split(mat * d_gap)
            yb, dyb = yb_ref[0, b, rows, :], yb_ref[1, b, rows, :]
            y_hi, y_lo = split(yb)
            dy_hi, dy_lo = split(dyb)
            got = mmt(jnp.concatenate([y_hi, dy_hi, y_lo, dy_lo], axis=0), l_hi)
            low = mmt(jnp.concatenate([y_hi, dy_hi], axis=0), l_lo)
            both = got[: 2 * HD] + got[2 * HD :] + low
            gap_part = mmt(jnp.concatenate([y_hi, y_lo], axis=0), n_hi)
            gap_part = gap_part[:HD] + gap_part[HD:] + mmt(y_hi, n_lo)
            xt = r_ref[b, rows, :]
            bl_i, dbl_i = bl[rows], dbl[rows]
            tail, dt, ddt, dc, dg = row(K_TAIL), row(K_DT), row(K_DDT), row(K_DC), row(K_DG)
            k = both[:HD] + tail * bl_i
            dk = both[HD:] + gap_part + tail * ((dg - dc) * bl_i + dbl_i)
            out_parts.append(ddt * k + dt * dk + row(K_DD) * yb + row(K_D) * dyb)
            y_nd, dy_nd = y_ref[0, b, rows, :], y_ref[1, b, rows, :]
            xk, dxk = head_sum(xt * k), head_sum(xt * dk)
            e0 = head_sum(yb * y_nd) - dt * xk
            e1 = head_sum(dyb * y_nd + yb * dy_nd) - ddt * xk - dt * dxk
            xbl, dxbl = head_sum(xt * bl_i), head_sum(xt * dbl_i)
            h, dh = hb_ref[b, 0, rows, :], hb_ref[b, 1, rows, :]
            lam, d_lam = adj[rows], d_adj[rows]
            eg = jnp.exp(row(K_G))
            hl = eg * head_sum(lam * h)
            dhl = eg * head_sum(d_lam * h + lam * dh)
            g0 = hl + row(K_W) * xbl
            g1 = dg * hl + dhl + row(K_DW) * xbl + row(K_W) * dxbl
            acc_a[i] = acc_a[i] + dc * e0 + row(K_C) * e1 + dg * g0 + row(K_G) * g1
            acc_dt[i] = (
                acc_dt[i] + row(K_DSG) * xk + row(K_SG) * dxk + row(K_F1) * e0 + row(K_F0) * e1
                + row(K_F1T) * g0 + row(K_F0T) * g1
            )
            acc_skip[i] = acc_skip[i] + head_sum(xt * dyb)
        out = jnp.concatenate(out_parts, axis=0)
        for i in range(CPD // 128):
            o_ref[b, i * 128 : (i + 1) * 128, :] = out[i * 128 : (i + 1) * 128].T
        if b:
            eg = jnp.exp(heads_rows(table_ref, K_G, b))
            d_adj = eg * (d_adj + heads_rows(table_ref, K_DG, b) * adj) + seed_ref[b, 1]
            adj = eg * adj + seed_ref[b, 0]
    sums = jnp.concatenate(acc_a + acc_dt + acc_skip + [jnp.zeros((T - 3 * HPD, T), F32)], axis=0)
    sums = jnp.sum(sums.T, axis=0, keepdims=True)
    part = jnp.concatenate([gain_ref[...], sums, jnp.zeros((PART - 3, T), F32)], axis=0)
    copies = []
    for d in range(BLK):
        copies.append(pltpu.make_async_copy(o_ref.at[lax.rem(zl_ref[0] + d, BLK)], o_refs[d], sems.at[d]))
        copies[-1].start()
    for i in range(NEAR):
        part_ref[i] = part
    for copy in copies:
        copy.wait()


def place_kernel(zl_ref, i0, i1, i2, i3, o_ref, sems):
    copies = []
    for d, src in enumerate((i0, i1, i2, i3)):
        j = lax.rem(zl_ref[0] + BLK - d, BLK)
        for i in range(CPD // 128):
            lo = pl.multiple_of(j * CPD + i * 128, 128)
            copies.append(
                pltpu.make_async_copy(
                    src.at[pl.ds(i * 128, 128), :], o_ref.at[:, pl.ds(lo, 128)], sems.at[len(copies)]
                )
            )
            copies[-1].start()
    for copy in copies:
        copy.wait()


def sum_kernel(m_ref, *rest):
    o_ref = rest[-1]
    total = m_ref[0]
    for i in range(1, NEAR):
        total = total + m_ref[i]
    for i in range(FAR):
        o_ref[i] = total


def finish_kernel(factor, m_ref, gain_ref, *head_refs):
    heads = []
    for j in range(BLK):
        total = m_ref[j]
        for i in range(1, FAR // BLK):
            total = total + m_ref[i * BLK + j]
        total = total * factor
        gain_ref[2 * j : 2 * j + 2, :] = total[0:2, :]
        heads.append(total[2:3, :])
    for n, ref in enumerate(head_refs):
        ref[...] = jnp.concatenate([v[:, n * HPD : (n + 1) * HPD] for v in heads], axis=1)


def call(kernel, name, outs, in_specs=None, scratch=(), out_specs=None):
    def shape(dims):
        return jax.ShapeDtypeStruct(dims, F32)

    many = isinstance(outs, list)
    spec = pl.BlockSpec(memory_space=pltpu.VMEM)

    def run(*args):
        return pl.pallas_call(
            kernel,
            name=name,
            out_shape=[shape(o) for o in outs] if many else shape(outs),
            out_specs=out_specs or ([spec] * len(outs) if many else spec),
            in_specs=in_specs or [spec] * len(args),
            scratch_shapes=list(scratch),
            compiler_params=pltpu.CompilerParams(vmem_limit_bytes=VMEM),
        )(*args)

    return run


def per_device(
    ssm_input,
    gate_input,
    b_proj,
    c_proj,
    dt_raw,
    cotangent,
    a_log,
    dt_bias,
    d_skip,
    norm_gain,
    probe_a,
    probe_dt,
    probe_skip,
    probe_gain,
):
    vm, sm, hbm = [pl.BlockSpec(memory_space=m) for m in (pltpu.VMEM, pltpu.SMEM, pltpu.HBM)]

    def in_hbm(v):
        return pltpu.with_memory_space_constraint(v, pltpu.HBM)

    def exchange(v, axes):
        return lax.all_to_all(v, axes, 0, 0)

    group, segs = "zl", ("zh", "y")

    def shift(v, d):
        return lax.ppermute(v, group, [(i, (i + d) % BLK) for i in range(BLK)])

    zl = lax.axis_index(group).reshape(1)
    params = jnp.stack([a_log, dt_bias, d_skip, probe_a, probe_dt, probe_skip])
    params = lax.dynamic_slice_in_dim(params, lax.axis_index(group) * HPD, HPD, 1)
    params = jnp.broadcast_to(params.reshape(PARAMS * HPD, 1), (PARAMS * HPD, T))
    gain = (norm_gain.reshape(8, 128), probe_gain.reshape(8, 128))
    packed = call(pack_x_kernel, "pack_x", (BLK, X_ROWS, T), [hbm] * 4,
        [pltpu.VMEM((T, CH), BF16), pltpu.VMEM((T, N), BF16), pltpu.VMEM((HEADS, T), F32), pltpu.VMEM((T, N), BF16)]
        + [pltpu.SemaphoreType.DMA((4,))],
    )(*[in_hbm(v) for v in (ssm_input, b_proj, dt_raw.T, c_proj)])
    r = exchange(packed, group)
    parts = call(pack_g_kernel, "pack_g", [(G_ROWS, T)] * BLK, [sm] + [vm] * 2,
        [pltpu.VMEM((G_ROWS, T), F32)] * BLK + [pltpu.SemaphoreType.DMA((BLK,))], [hbm] * BLK,
    )(zl, gate_input, cotangent)
    parts = [shift(v, d) if d else v for d, v in enumerate(parts)]
    table, s, msg = call(
        state_kernel,
        "state",
        [(TABLE, ROWS, T), (BLK, 2, CPD, N), (SEGS, M_ROWS, N)],
        [vm, vm] + [hbm] * len(FIRST),
    )(params, r, *[parts[d] for d in FIRST])
    decay = exchange(msg, segs)
    early = [parts[d] for d in EARLY]
    before = call(scan_up_kernel, "scan_up", (SEGS, 2 * CPS, N), [vm] + [hbm] * len(early))(decay, *early)
    h_in = exchange(before, segs)
    g, y, h_blocks, norms = call(
        out_kernel,
        "mix",
        [(BLK, G_ROWS, T), (2, BLK, CPD, T), (BLK, 2, CPD, N), (BLK, 4 * BLK, T)],
        [sm] + [vm] * 3 + [hbm] * BLK + [vm] * 3,
        [pltpu.SemaphoreType.DMA((BLK,))],
    )(zl, *gain, r, *[in_hbm(v) for v in parts], h_in, table, s)
    norms = exchange(norms, group)
    y_bar, seeds, d_gain, msg = call(
        seed_kernel,
        "seeds",
        [(2, BLK, CPD, T), (BLK, 2, CPD, N), (2, 128), (SEGS, 2 * CPS, N)],
        [sm] + [vm] * 7,
    )(zl, *gain, r, g, norms, table, y)
    after = call(functools.partial(scan_kernel, True), "scan_down", (SEGS, 2 * CPS, N))(
        decay, exchange(msg, segs)
    )
    adj = exchange(after, segs)
    *outs, part = call(
        input_kernel,
        "input_grad",
        [(CPD, 128)] * BLK + [(NEAR, PART, T)],
        [sm] + [vm] * 9,
        [pltpu.VMEM((BLK, CPD, 128), F32), pltpu.SemaphoreType.DMA((BLK,))],
        [hbm] * BLK + [vm],
    )(zl, r, g, adj, table, y, y_bar, h_blocks, seeds, d_gain)
    outs = [shift(v, d) if d else v for d, v in enumerate(outs)]
    part = exchange(part, ("x", "core", "y"))
    early = [outs[d] for d in BACK]
    part = call(sum_kernel, "near_sum", (FAR, PART, T), [vm] + [hbm] * len(early))(part, *early)
    hvp_input = call(
        place_kernel,
        "place",
        (T, CH),
        [sm] + [hbm] * BLK,
        [pltpu.SemaphoreType.DMA((CH // 128,))],
        hbm,
    )(zl, *outs)
    factor = 1.0 / math.sqrt(T * NEAR * FAR)
    hvp_gain, *heads = call(functools.partial(finish_kernel, factor), "finish", [(8, 128)] + [(1, HEADS)] * 3)(
        exchange(part, ("zhi", "zh", "zl"))
    )
    return (
        hvp_input,
        *[v.reshape(HEADS) for v in heads],
        hvp_gain.reshape(CH),
    )


def solution(mesh):
    axes = ("zhi", "x", "core", "y", "zh", "zl")
    fine = Mesh(mesh.devices.reshape(2, 4, 2, 4, 2, 4), axes)
    tokens = P(axes, None)
    return jax.shard_map(
        per_device,
        mesh=fine,
        in_specs=(tokens,) * 6 + (P(),) * 8,
        out_specs=(tokens, P(), P(), P(), P()),
        check_vma=False,
    )
```
